32 devices in a mesh: src: 8 (over z, core), rcv: 4 (over y, x).
Axes of the slice: x: 2, y: 2, z: 4, core: 2. Of those that a mesh axis runs over, the one named last changes fastest.
Arguments:
- flows: float32 [24, 1024], P(None, 'src'), may hold values from 0.05 to 2
- speeds: float32 [24, 1024], P(None, 'src'), may hold values from 0.3 to 1.2
- seg_length: float32 [8192], P('src'), may hold values from 10 to 100
- relay_list: int32 [8, 8, 16], P('src'), may hold values from -1 to 127, as said below
- seg_slot: int32 [8192], P('src'), may hold values from 0 to 127, as said below
- tile_pairs: int32 [8, 4, 2, 12], P('src', 'rcv'), may hold values from 0 to 7, as said below
- tile_count: int32 [8, 4], P('src', 'rcv'), may hold values from 2 to 12, as said below
- attenuation: bfloat16 [8, 4, 12, 8, 128, 128], P('src', 'rcv')
- dwellings: int32 [4096], P('rcv'), may hold values from 1 to 22
Outputs:
- grad_flows: float32 [24, 1024], P(None, 'src')
- grad_speeds: float32 [24, 1024], P(None, 'src')
- annoyed_count: float32 [], replicated
The draws below stay inside these ranges and needn't reach their ends.
Inputs may be any that keep to these rules, and one draw needn't show every extreme that they name: relay_list[d, o, :] holds distinct local link indices of owner o first and -1 after them; from 8 to 16 of them are live, and for every d at least one owner has all 16 live. `seg_slot`: each segment's slot names a live entry of its own block's relay list, and every live entry is named by some segment of that block. `tile_pairs`: entry 0 is a segment block below 8, entry 1 a facade block below 8; the pairs of one device are distinct. Only the first tile_count slots of a device are live; some device has all 12 live.
All inputs are finite; a program needn't handle non-finite values.
Results may differ from the reference program's by a relative error of at most 0.0005.
Values may be sent and summed in bfloat16 or wider, within the bound.
No kernel may reach another device: no remote copies, remote signals or barrier semaphores. Data moves between devices by JAX's collectives and lax.ppermute only.
A program may use at most 64 MiB of HBM per device.

```python
import math
import jax
import jax.numpy as jnp
from jax import lax

HOURS = 24
BANDS = 8
BLK = 128
TILES_DEV = 12
CAP = 16
S_DEV = 1024
R_DEV = 1024
L_DEV = 128
SEGS = 8192
LINKS = 1024
N_SRC = 8
N_RCV = 4


def relay_tables(key):
    base_key = jax.random.fold_in(key, 11)
    key_count, key_perm, key_offset, key_pick, key_order = jax.random.split(base_key, 5)
    counts = jax.random.randint(key_count, (N_SRC, N_SRC), (CAP + 1) // 2, CAP + 1)
    offset = jax.random.randint(key_offset, (N_SRC,), 0, N_SRC)
    destination = jnp.arange(N_SRC, dtype=jnp.int32)[:, None]
    owner_index = jnp.arange(N_SRC, dtype=jnp.int32)[None, :]
    counts = jnp.where(owner_index == (destination + offset[:, None]) % N_SRC, CAP, counts)
    key_list = jax.random.split(key_perm, N_SRC * N_SRC)
    link_perm = jax.vmap(lambda single: jax.random.permutation(single, L_DEV)[:CAP])(key_list)
    link_perm = link_perm.reshape(N_SRC, N_SRC, CAP)
    position = jnp.arange(CAP, dtype=jnp.int32)[None, None, :]
    is_live = position < counts[:, :, None]
    relay_table = jnp.where(is_live, link_perm, -1).astype(jnp.int32)
    live_flat = is_live.reshape(N_SRC, N_SRC * CAP).astype(jnp.int32)
    ordering = jnp.argsort(1 - live_flat, axis=1, stable=True)
    live_total = jnp.sum(live_flat, axis=1)
    seg_position = jnp.arange(S_DEV, dtype=jnp.int32)[None, :]
    extra_pick = jax.random.randint(key_pick, (N_SRC, S_DEV), 0, live_total[:, None])
    pick_index = jnp.where(seg_position < live_total[:, None], seg_position, extra_pick)
    slot_ids = jnp.take_along_axis(ordering, pick_index, axis=1)
    seg_keys = jax.random.split(key_order, N_SRC)
    seg_perm = jax.vmap(lambda single: jax.random.permutation(single, S_DEV))(seg_keys)
    slot_ids = jnp.take_along_axis(slot_ids, seg_perm, axis=1)
    return (relay_table, slot_ids.reshape(-1).astype(jnp.int32))


def draw_relay_list(key, part):
    return relay_tables(key)[0]


def draw_seg_slot(key, part):
    return relay_tables(key)[1]


def draw_tile_pairs(key, part):
    grid_tiles = S_DEV // BLK * (R_DEV // BLK)
    row_blocks = R_DEV // BLK
    key_list = jax.random.split(jax.random.fold_in(key, 23), N_SRC * N_RCV)
    chosen = jax.vmap(lambda single: jax.random.permutation(single, grid_tiles)[:TILES_DEV])(key_list)
    tile_list = jnp.stack([chosen // row_blocks, chosen % row_blocks], axis=1)
    return tile_list.reshape(N_SRC, N_RCV, 2, TILES_DEV).astype(jnp.int32)


def draw_tile_count(key, part):
    key_first, key_second, key_busy = jax.random.split(jax.random.fold_in(key, 31), 3)
    spread = TILES_DEV - 2
    first_draw = jax.random.randint(key_first, (N_SRC, N_RCV), 0, spread + 1)
    second_draw = jax.random.randint(key_second, (N_SRC, N_RCV), 0, spread + 1)
    counts = 2 + first_draw * second_draw // spread
    busiest = jax.random.randint(key_busy, (), 0, N_SRC * N_RCV)
    flat_index = jnp.arange(N_SRC * N_RCV, dtype=jnp.int32).reshape(N_SRC, N_RCV)
    return jnp.where(flat_index == busiest, TILES_DEV, counts).astype(jnp.int32)


def draw_attenuation(key, part):
    key_tile = jax.random.fold_in(jax.random.fold_in(key, 41), 0)
    key_entry = jax.random.fold_in(jax.random.fold_in(key, 41), 1)
    key_source = jax.random.fold_in(jax.random.fold_in(key, 41), 3)
    key_facade = jax.random.fold_in(jax.random.fold_in(key, 41), 4)
    full_shape = (N_SRC, N_RCV, TILES_DEV, BANDS, BLK, BLK)
    tile_scale = jnp.exp(jax.random.uniform(key_tile, (N_SRC, N_RCV, TILES_DEV, 1, 1, 1), jnp.float32, math.log(0.001), 0.0))
    band_scale = jnp.exp(-0.1 * math.log(10.0) * jnp.arange(BANDS, dtype=jnp.float32)).reshape(1, 1, 1, BANDS, 1, 1)
    source_place = jax.random.uniform(key_source, (N_SRC, N_RCV, TILES_DEV, 1, BLK, 1), jnp.float32, 0.0, 1.0)
    facade_place = jax.random.uniform(key_facade, (N_SRC, N_RCV, TILES_DEV, 1, 1, BLK), jnp.float32, 0.0, 1.0)
    apart = (source_place - facade_place) / 0.05
    spreading = 1.0 / (1.0 + apart * apart)
    roughness = jnp.exp(jax.random.uniform(key_entry, full_shape, jnp.float32, math.log(0.3), math.log(3.0)))
    return (0.002 * tile_scale * band_scale * spreading * roughness).astype(jnp.bfloat16)


def draw_dwellings(key, part):
    position = jnp.arange(R_DEV * N_RCV, dtype=jnp.int32)
    inside = position % R_DEV
    block_index = position // R_DEV
    upper = 2 + 12 * inside // R_DEV + 12 * block_index // N_RCV
    values = 1 + jax.random.randint(jax.random.fold_in(key, 53), (R_DEV * N_RCV,), 0, upper)
    values = jnp.where(position == R_DEV * N_RCV - 1, upper, values)
    return values.astype(jnp.int32)


def shard_levels(rng, shape, pieces, smallest, high):
    level, own = 1.0, jax.random.fold_in(rng, 6)
    for axis_at, shards_of in pieces:
        steps = jnp.exp(jax.random.uniform(jax.random.fold_in(own, axis_at), (shards_of,), jnp.float32, smallest / len(pieces), high / len(pieces)))
        level = level * jnp.repeat(steps, shape[axis_at] // shards_of).reshape([-1 if axis == axis_at else 1 for axis in range(len(shape))])
    return level


def setup_inputs(seed: int = 0) -> dict:
    arg_keys = jax.random.split(jax.random.key(seed), 10)
    return {
        "flows": jnp.clip(jnp.exp(math.log(2.0) - 3.6888794 * jax.random.uniform(arg_keys[0], (HOURS, LINKS), jnp.float32) ** shard_levels(arg_keys[0], (HOURS, LINKS), ((1, 8),), -0.2, 0.2)), 0.05, 2.0),
        "speeds": jnp.clip(jnp.exp(math.log(1.2) - 1.3862944 * jax.random.uniform(arg_keys[1], (HOURS, LINKS), jnp.float32) ** shard_levels(arg_keys[1], (HOURS, LINKS), ((1, 8),), -0.2, 0.2)), 0.3, 1.2),
        "seg_length": jnp.clip(jnp.exp(math.log(100.0) - 2.3025851 * jax.random.uniform(arg_keys[2], (SEGS,), jnp.float32) ** shard_levels(arg_keys[2], (SEGS,), ((0, 8),), -0.2, 0.2)), 10.0, 100.0),
        "relay_list": draw_relay_list(jax.random.fold_in(arg_keys[9], 71), 0),
        "seg_slot": draw_seg_slot(jax.random.fold_in(arg_keys[9], 71), 0),
        "tile_pairs": draw_tile_pairs(jax.random.fold_in(arg_keys[9], 71), 0),
        "tile_count": draw_tile_count(jax.random.fold_in(arg_keys[9], 71), 0),
        "attenuation": draw_attenuation(jax.random.fold_in(arg_keys[9], 71), 0),
        "dwellings": draw_dwellings(jax.random.fold_in(arg_keys[9], 71), 0),
    }


rolling_base = [79.7, 85.7, 84.5, 90.2, 97.3, 93.9, 84.1, 74.3]
rolling_slope = [30.0, 41.5, 38.9, 25.7, 32.5, 37.2, 39.0, 40.0]
propel_base = [94.5, 89.2, 88.0, 85.9, 84.2, 86.9, 83.3, 76.1]
propel_slope = [-1.3, 7.2, 7.7, 8.0, 8.0, 8.0, 8.0, 8.0]
aweight_db = [-26.2, -16.1, -8.6, -3.2, 0.0, 1.2, 1.0, -1.1]

def band_column(values):
    return jnp.asarray(values, dtype=jnp.float32)[:, None, None]

def emission(seg_flow, seg_speed, seg_length):
    decibel = math.log(10.0) / 10.0
    speed_kmh = 100.0 * seg_speed
    log_ratio = jnp.log10(speed_kmh / 70.0)
    rolling = jnp.exp(decibel * (band_column(rolling_base) - 90.0 + band_column(rolling_slope) * log_ratio[None]))
    propel = jnp.exp(decibel * (band_column(propel_base) - 90.0 + band_column(propel_slope) * (speed_kmh[None] - 70.0) / 70.0))
    factor = seg_length[None, :] * seg_flow / (100.0 * seg_speed)
    seg_power = factor[None] * (rolling + propel)
    seg_slope = factor[None] * (rolling * (band_column(rolling_slope) / 10.0 - 1.0) / seg_speed[None] + propel * (math.log(10.0) * band_column(propel_slope) / 7.0 - 1.0 / seg_speed[None]))
    return (seg_power, seg_slope)

def band_weight():
    return jnp.exp(math.log(10.0) / 10.0 * band_column(aweight_db))

def dose_response(energy, dwell):
    hour_index = jnp.arange(energy.shape[0], dtype=jnp.int32)
    hour_weight = jnp.where((hour_index >= 7) & (hour_index < 19), 1.0, jnp.where((hour_index >= 19) & (hour_index < 23), math.sqrt(10.0), 10.0)).astype(jnp.float32)
    weighted_sum = lax.optimization_barrier(jnp.sum(hour_weight[:, None] * (energy + 0.01), axis=0))
    lden_level = 60.0 + 10.0 * jnp.log10(weighted_sum / 24.0)
    people = dwell.astype(jnp.float32)
    annoyed = people * (78.927 - 3.1162 * lden_level + 0.0342 * lden_level * lden_level) / 100.0
    level_slope = people * (-3.1162 + 0.0684 * lden_level) / 100.0 * (10.0 / math.log(10.0))
    level_grad = (level_slope / weighted_sum)[None, :] * hour_weight[:, None]
    return (jnp.sum(annoyed), level_grad)

def reference(flows, speeds, seg_length, relay_list, seg_slot, tile_pairs, tile_count, attenuation, dwellings):
    segment_dev = jnp.arange(N_SRC * S_DEV, dtype=jnp.int32) // S_DEV
    owner_dev = seg_slot // CAP
    within = seg_slot % CAP
    link_index = (owner_dev * L_DEV + relay_list[segment_dev, owner_dev, within]).astype(jnp.int32)
    seg_flow = flows[:, link_index]
    seg_speed = speeds[:, link_index]
    seg_power, seg_slope = emission(seg_flow, seg_speed, seg_length)
    weighted = (band_weight() * seg_power).astype(jnp.bfloat16)
    device_list = jnp.arange(N_SRC * N_RCV, dtype=jnp.int32)
    tile_steps = jnp.arange(TILES_DEV, dtype=jnp.int32)

    def forward_device(energy, device):
        src_index = device // N_RCV
        rcv_index = device % N_RCV
        tile_list = tile_pairs[src_index, rcv_index]
        live_tiles = tile_count[src_index, rcv_index]
        tile_data = attenuation[src_index, rcv_index]

        def forward_tile(energy, tile_step):
            seg_start = (src_index * S_DEV + tile_list[0, tile_step] * BLK).astype(jnp.int32)
            rcv_start = (rcv_index * R_DEV + tile_list[1, tile_step] * BLK).astype(jnp.int32)
            block = lax.dynamic_slice_in_dim(weighted, seg_start, BLK, 2).astype(jnp.float32)
            tile = tile_data[tile_step].astype(jnp.float32)
            contrib = jnp.einsum('bhs,bsr->hr', block, tile, precision=lax.Precision.HIGHEST)
            contrib = jnp.where(tile_step < live_tiles, contrib, 0.0)
            previous = lax.dynamic_slice_in_dim(energy, rcv_start, BLK, 1)
            return (lax.dynamic_update_slice_in_dim(energy, previous + contrib, rcv_start, 1), None)
        energy, _ = lax.scan(forward_tile, energy, tile_steps)
        return (energy, None)
    energy, _ = lax.scan(forward_device, jnp.zeros((HOURS, N_RCV * R_DEV), jnp.float32), device_list)
    annoyed_count, level_grad = dose_response(energy, dwellings)
    level_grad = level_grad.astype(jnp.bfloat16)

    def backward_device(seg_back, device):
        src_index = device // N_RCV
        rcv_index = device % N_RCV
        tile_list = tile_pairs[src_index, rcv_index]
        live_tiles = tile_count[src_index, rcv_index]
        tile_data = attenuation[src_index, rcv_index]

        def backward_tile(seg_back, tile_step):
            seg_start = (src_index * S_DEV + tile_list[0, tile_step] * BLK).astype(jnp.int32)
            rcv_start = (rcv_index * R_DEV + tile_list[1, tile_step] * BLK).astype(jnp.int32)
            grad_block = lax.dynamic_slice_in_dim(level_grad, rcv_start, BLK, 1).astype(jnp.float32)
            tile = tile_data[tile_step].astype(jnp.float32)
            contrib = jnp.einsum('hr,bsr->bhs', grad_block, tile, precision=lax.Precision.HIGHEST)
            contrib = jnp.where(tile_step < live_tiles, contrib, 0.0)
            previous = lax.dynamic_slice_in_dim(seg_back, seg_start, BLK, 2)
            return (lax.dynamic_update_slice_in_dim(seg_back, previous + contrib, seg_start, 2), None)
        seg_back, _ = lax.scan(backward_tile, seg_back, tile_steps)
        return (seg_back, None)
    seg_back, _ = lax.scan(backward_device, jnp.zeros((BANDS, HOURS, N_SRC * S_DEV), jnp.float32), device_list)
    flow_part = lax.optimization_barrier(jnp.sum(band_weight() * seg_back * seg_power, axis=0)) / seg_flow
    speed_part = lax.optimization_barrier(jnp.sum(band_weight() * seg_back * seg_slope, axis=0))
    grad_flows = jnp.zeros((HOURS, N_SRC * L_DEV), jnp.float32).at[:, link_index].add(flow_part)
    grad_speeds = jnp.zeros((HOURS, N_SRC * L_DEV), jnp.float32).at[:, link_index].add(speed_part)
    return (grad_flows, grad_speeds, annoyed_count)
```

```python
import functools
import math

import jax
import jax.numpy as jnp
from jax import lax
from jax.experimental import pallas as pl
from jax.experimental.pallas import tpu as pltpu
from jax.sharding import PartitionSpec as P

rolling_base = [79.7, 85.7, 84.5, 90.2, 97.3, 93.9, 84.1, 74.3]
rolling_slope = [30.0, 41.5, 38.9, 25.7, 32.5, 37.2, 39.0, 40.0]
propel_base = [94.5, 89.2, 88.0, 85.9, 84.2, 86.9, 83.3, 76.1]
propel_slope = [-1.3, 7.2, 7.7, 8.0, 8.0, 8.0, 8.0, 8.0]
aweight_db = [-26.2, -16.1, -8.6, -3.2, 0.0, 1.2, 1.0, -1.1]

BANDS = 8
LANES = 128
CLASSES = 3
ROOT = math.sqrt(10.0)
DECIBEL = math.log(10.0) / 10.0
NT = (((1,), (1,)), ((), ()))


def iota(shape, axis):
    return lax.broadcasted_iota(jnp.int32, shape, axis)


def hour_class(shape):
    hour = iota(shape, 0)
    day = (hour >= 7) & (hour < 19)
    evening = (hour >= 19) & (hour < 23)
    return jnp.where(day, 0, jnp.where(evening, 1, 2))


def band_terms(band, speed_kmh, log_ratio):
    shift = aweight_db[band] - 90.0
    rolling = jnp.exp(
        DECIBEL * (rolling_base[band] + shift) + (DECIBEL * rolling_slope[band]) * log_ratio
    )
    propel = jnp.exp(
        DECIBEL * (propel_base[band] + shift)
        + (DECIBEL * propel_slope[band] / 70.0) * (speed_kmh - 70.0)
    )
    return rolling, propel


def lane_pick(table, index):
    return jnp.take_along_axis(table, index, axis=1, mode="promise_in_bounds")


def swap_groups(block):
    row, lane = iota((8, LANES), 0), iota((8, LANES), 1)
    block = lane_pick(block, (lane + LANES - 16 * row) % LANES)
    block = jnp.take_along_axis(
        block, (lane // 16 + 8 - row) % 8, axis=0, mode="promise_in_bounds"
    )
    return lane_pick(block, (lane + 16 * row) % LANES)


def split2(value):
    high = value.astype(jnp.bfloat16)
    low = (value - high.astype(jnp.float32)).astype(jnp.bfloat16)
    return high, low


def source_kernel(copies, flow_ref, speed_ref, out_ref):
    flow, speed = flow_ref[...], speed_ref[...]
    kind = hour_class(flow.shape)
    weight = jnp.where(kind == 0, 1.0, jnp.where(kind == 1, ROOT, 10.0))
    speed_kmh = 100.0 * speed
    log_ratio = jnp.log(speed_kmh / 70.0) * (1.0 / math.log(10.0))
    scale = weight * flow / speed_kmh
    row = iota((BANDS, LANES), 0)
    result = jnp.zeros((BANDS, LANES), jnp.float32)
    for band in range(BANDS):
        rolling, propel = band_terms(band, speed_kmh, log_ratio)
        total = jnp.sum(scale * (rolling + propel), axis=0, keepdims=True)
        result = jnp.where(row == band, total, result)
    for copy in range(copies):
        out_ref[copy * BANDS : (copy + 1) * BANDS] = result


def table_kernel(flow_ref, speed_ref, slot_ref, flow_table, speed_table, spread_ref):
    flow, speed = flow_ref[...], speed_ref[...]
    speed_kmh = 100.0 * speed
    log_ratio = jnp.log(speed_kmh / 70.0) * (1.0 / math.log(10.0))
    per_flow = 1.0 / speed_kmh
    factor = flow * per_flow
    inverse = 1.0 / speed
    for band in range(BANDS):
        rolling, propel = band_terms(band, speed_kmh, log_ratio)
        flow_table[band] = per_flow * (rolling + propel)
        speed_table[band] = factor * (
            rolling * (rolling_slope[band] / 10.0 - 1.0) * inverse
            + propel * (math.log(10.0) * propel_slope[band] / 7.0 - inverse)
        )
    blocks = slot_ref.shape[0]
    slots = spread_ref.shape[0]
    for block in range(blocks):
        same = iota((slots, LANES), 0) == slot_ref[block : block + 1]
        spread_ref[:, block * LANES : (block + 1) * LANES] = jnp.where(
            same, 1.0, 0.0
        ).astype(jnp.bfloat16)


def forward_kernel(
    copies, pairs_ref, count_ref, link_ref, relay_ref, slot_ref, length_ref, tile_ref, out_ref,
    seg_scratch, acc_scratch,
):
    owners = link_ref.shape[0] // BANDS
    groups = owners // 8
    lane = iota((BANDS, LANES), 1)
    tables = []
    for group in range(groups):
        index = jnp.broadcast_to(relay_ref[group : group + 1], (BANDS, LANES))
        index = jnp.maximum(index, 0)
        table = jnp.zeros((BANDS, LANES), jnp.float32)
        for member in range(8):
            owner = group * 8 + member
            picked = lane_pick(link_ref[owner * BANDS : (owner + 1) * BANDS], index)
            table = jnp.where(lane // 16 == member, picked, table)
        tables.append(table)
    blocks = slot_ref.shape[0]
    for block in range(blocks):
        slot = jnp.broadcast_to(slot_ref[block : block + 1], (BANDS, LANES))
        value = lane_pick(tables[0], slot % LANES)
        for group in range(1, groups):
            value = jnp.where(slot // LANES == group, lane_pick(tables[group], slot % LANES), value)
        high, low = split2(value * length_ref[block : block + 1])
        seg_scratch[block] = jnp.concatenate([high, low], axis=0)
    acc_scratch[...] = jnp.zeros(acc_scratch.shape, jnp.float32)
    row = iota((2 * BANDS, LANES), 0) % BANDS

    def tile(step, carry):
        seg = seg_scratch[pairs_ref[0, step]]
        facade = pairs_ref[1, step]
        rows = jnp.concatenate(
            [jnp.where(row == band, seg, jnp.zeros_like(seg)) for band in range(BANDS)], axis=1
        )
        tiles = tile_ref[step].reshape(BANDS * LANES, LANES)
        acc_scratch[facade] += jnp.dot(rows, tiles, preferred_element_type=jnp.float32)
        return carry

    lax.fori_loop(0, count_ref[0, 0], tile, 0)
    facades = acc_scratch.shape[0]
    sums = [jnp.sum(acc_scratch[block], axis=0, keepdims=True) for block in range(facades)]
    result = jnp.concatenate(sums, axis=0)
    for copy in range(copies):
        out_ref[copy * facades : (copy + 1) * facades] = result


def backward_kernel(
    hours_weight, receivers, pairs_ref, count_ref, part_ref, people_ref, relay_ref, length_ref,
    spread_ref, tile_ref, out_ref, grad_scratch, acc_scratch,
):
    facades = people_ref.shape[0]
    sources = part_ref.shape[0] // facades
    total = part_ref[0:facades]
    for source in range(1, sources):
        total = total + part_ref[source * facades : (source + 1) * facades]
    total = total + 0.01 * hours_weight
    level = 60.0 + (10.0 / math.log(10.0)) * jnp.log(total / 24.0)
    people = people_ref[...].astype(jnp.float32)
    annoyed = people * (78.927 - 3.1162 * level + 0.0342 * level * level) / 100.0
    annoyed = jnp.sum(annoyed, keepdims=True)
    slope = people * (-3.1162 + 0.0684 * level) / 100.0 * (10.0 / math.log(10.0)) / total
    grads = [slope, slope * ROOT, slope * 10.0]
    pad = jnp.zeros((8, LANES), jnp.float32)
    for block in range(facades):
        rows = [jnp.broadcast_to(g[block : block + 1], (BANDS, LANES)) for g in grads]
        grad_scratch[block] = jnp.concatenate(rows + [pad], axis=0).astype(jnp.bfloat16)
    acc_scratch[...] = jnp.zeros(acc_scratch.shape, jnp.float32)
    row = iota((32, LANES), 0) % BANDS

    def tile(step, carry):
        block = pairs_ref[0, step]
        grad = grad_scratch[pairs_ref[1, step]]
        acc = acc_scratch[block]
        for band in range(BANDS):
            acc = acc + lax.dot_general(
                jnp.where(row == band, grad, jnp.zeros_like(grad)),
                tile_ref[step, band],
                NT,
                preferred_element_type=jnp.float32,
            )
        acc_scratch[block] = acc
        return carry

    lax.fori_loop(0, count_ref[0, 0], tile, 0)
    used = CLASSES * BANDS
    blocks = acc_scratch.shape[0]
    high, low = [], []
    for block in range(blocks):
        value = acc_scratch[block][:used] * length_ref[block : block + 1]
        high_part = value.astype(jnp.bfloat16).astype(jnp.float32)
        high.append(high_part)
        low.append(value - high_part)
    rows = jnp.concatenate(
        [jnp.concatenate(high, axis=1), jnp.concatenate(low, axis=1)], axis=0
    ).astype(jnp.bfloat16)
    slots = lax.dot_general(rows, spread_ref[...], NT, preferred_element_type=jnp.float32)
    slots = slots[:used] + slots[used:]
    owners = out_ref.shape[0] // receivers
    row8, lane8 = iota((8, LANES), 0), iota((8, LANES), 1)
    for group in range(owners // 8):
        lanes = slice(group * LANES, (group + 1) * LANES)
        rows = [
            swap_groups(slots[kind * BANDS : (kind + 1) * BANDS, lanes])
            for kind in range(CLASSES)
        ]
        relay = relay_ref[group * 8 : (group + 1) * 8].astype(jnp.float32)
        for receiver in range(receivers):
            first = receiver * owners + group * 8
            for kind in range(CLASSES):
                out_ref[first : first + 8, kind * LANES : (kind + 1) * LANES] = rows[kind]
            out_ref[first : first + 8, CLASSES * LANES : (CLASSES + 1) * LANES] = relay
            out_ref[first : first + 8, (CLASSES + 1) * LANES :] = jnp.broadcast_to(
                annoyed, (8, LANES)
            )


def finish_kernel(receivers, in_ref, flow_table, speed_table, flow_out, speed_out, count_out):
    owners = in_ref.shape[0] // receivers
    count = in_ref[0:1, (CLASSES + 1) * LANES :]
    for receiver in range(1, receivers):
        first = receiver * owners
        count = count + in_ref[first : first + 1, (CLASSES + 1) * LANES :]
    count_out[...] = count
    row8, lane8 = iota((8, LANES), 0), iota((8, LANES), 1)
    used = CLASSES * BANDS
    links = jnp.zeros((2 * used, LANES), jnp.float32)
    for group in range(owners // 8):
        parts = []
        for kind in range(CLASSES):
            lanes = slice(kind * LANES, (kind + 1) * LANES)
            total = in_ref[group * 8 : group * 8 + 8, lanes]
            for receiver in range(1, receivers):
                first = receiver * owners + group * 8
                total = total + in_ref[first : first + 8, lanes]
            parts.append(swap_groups(total))
        value = jnp.concatenate(parts, axis=0)
        high = value.astype(jnp.bfloat16).astype(jnp.float32)
        rows = jnp.concatenate([high, value - high], axis=0).astype(jnp.bfloat16)
        relay = in_ref[group * 8 : group * 8 + 8, CLASSES * LANES : (CLASSES + 1) * LANES]
        relay = jnp.sum(jnp.where(lane8 // 16 == row8, relay, 0.0), axis=0, keepdims=True)
        relay = relay.astype(jnp.int32)
        spread = jnp.where(iota((LANES, LANES), 0) == relay, 1.0, 0.0).astype(jnp.bfloat16)
        links = links + lax.dot_general(rows, spread, NT, preferred_element_type=jnp.float32)
    links = links[:used] + links[used:]
    kind = hour_class(flow_out.shape)
    flow_sum = jnp.zeros(flow_out.shape, jnp.float32)
    speed_sum = jnp.zeros(flow_out.shape, jnp.float32)
    for band in range(BANDS):
        day, evening, night = [links[k * BANDS + band][None] for k in range(CLASSES)]
        back = jnp.where(kind == 0, day, jnp.where(kind == 1, evening, night))
        flow_sum = flow_sum + back * flow_table[band]
        speed_sum = speed_sum + back * speed_table[band]
    flow_out[...] = flow_sum
    speed_out[...] = speed_sum


def shards(
    flows, speeds, seg_length, relay_list, seg_slot, tile_pairs, tile_count, attenuation, dwellings
):
    sources, receivers = lax.axis_size("src"), lax.axis_size("rcv")
    hours = flows.shape[0]
    width = relay_list.shape[2]
    slots = sources * width
    tile_count_max = attenuation.shape[2]
    f32 = jnp.float32
    blocks, facades = seg_slot.shape[0] // LANES, dwellings.shape[0] // LANES
    hours_weight = sum(
        1.0 if 7 <= h < 19 else (ROOT if 19 <= h < 23 else 10.0) for h in range(hours)
    )
    vmem = pl.BlockSpec(memory_space=pltpu.VMEM)
    smem = pl.BlockSpec(memory_space=pltpu.SMEM)
    tiles = attenuation[0, 0]
    pairs = tile_pairs[0, 0]
    slot_rows = seg_slot.reshape(blocks, LANES)
    length_rows = seg_length.reshape(blocks, LANES)
    people = dwellings.reshape(facades, LANES)
    relay_rows = relay_list[0].reshape(slots // LANES, LANES)
    relay_wide = jnp.tile(relay_list[0], (1, LANES // width))

    power = pl.pallas_call(
        functools.partial(source_kernel, sources),
        out_shape=jax.ShapeDtypeStruct((sources * BANDS, LANES), f32),
        in_specs=[vmem, vmem],
        out_specs=vmem,
        name="source",
    )(flows, speeds)
    power = lax.all_to_all(power, "src", 0, 0, tiled=True)
    flow_table, speed_table, spread = pl.pallas_call(
        table_kernel,
        out_shape=[
            jax.ShapeDtypeStruct((BANDS, hours, LANES), f32),
            jax.ShapeDtypeStruct((BANDS, hours, LANES), f32),
            jax.ShapeDtypeStruct((slots, blocks * LANES), jnp.bfloat16),
        ],
        in_specs=[vmem] * 3,
        out_specs=[vmem] * 3,
        name="tables",
    )(flows, speeds, slot_rows)
    part = pl.pallas_call(
        functools.partial(forward_kernel, sources),
        out_shape=jax.ShapeDtypeStruct((sources * facades, LANES), f32),
        in_specs=[smem, smem] + [vmem] * 5,
        out_specs=vmem,
        scratch_shapes=[
            pltpu.VMEM((blocks, 2 * BANDS, LANES), jnp.bfloat16),
            pltpu.VMEM((facades, 2 * BANDS, LANES), f32),
        ],
        name="forward",
    )(pairs, tile_count, power, relay_rows, slot_rows, length_rows, tiles)
    part = lax.all_to_all(part, "src", 0, 0, tiled=True)
    back = pl.pallas_call(
        functools.partial(backward_kernel, hours_weight, receivers),
        out_shape=jax.ShapeDtypeStruct((receivers * sources, (CLASSES + 2) * LANES), f32),
        in_specs=[smem, smem] + [vmem] * 6,
        out_specs=vmem,
        scratch_shapes=[
            pltpu.VMEM((facades, 32, LANES), jnp.bfloat16),
            pltpu.VMEM((blocks, 32, LANES), f32),
        ],
        name="backward",
    )(pairs, tile_count, part, people, relay_wide, length_rows, spread, tiles)
    back = lax.all_to_all(back, ("rcv", "src"), 0, 0, tiled=True)
    grad_flows, grad_speeds, count = pl.pallas_call(
        functools.partial(finish_kernel, receivers),
        out_shape=[
            jax.ShapeDtypeStruct((hours, LANES), f32),
            jax.ShapeDtypeStruct((hours, LANES), f32),
            jax.ShapeDtypeStruct((1, LANES), f32),
        ],
        in_specs=[vmem] * 3,
        out_specs=[vmem] * 3,
        name="finish",
    )(back, flow_table, speed_table)
    return grad_flows, grad_speeds, count[0, 0]


def solution(mesh):
    in_specs = (
        P(None, "src"),
        P(None, "src"),
        P("src"),
        P("src", None, None),
        P("src"),
        P("src", "rcv", None, None),
        P("src", "rcv"),
        P("src", "rcv", None, None, None, None),
        P("rcv"),
    )
    out_specs = (P(None, "src"), P(None, "src"), P())
    return jax.shard_map(shards, mesh=mesh, in_specs=in_specs, out_specs=out_specs, check_vma=False)
```

```python
import functools
import math

import jax
import jax.numpy as jnp
from jax import lax
from jax.experimental import pallas as pl
from jax.experimental.pallas import tpu as pltpu
from jax.sharding import PartitionSpec as P

rolling_base = [79.7, 85.7, 84.5, 90.2, 97.3, 93.9, 84.1, 74.3]
rolling_slope = [30.0, 41.5, 38.9, 25.7, 32.5, 37.2, 39.0, 40.0]
propel_base = [94.5, 89.2, 88.0, 85.9, 84.2, 86.9, 83.3, 76.1]
propel_slope = [-1.3, 7.2, 7.7, 8.0, 8.0, 8.0, 8.0, 8.0]
aweight_db = [-26.2, -16.1, -8.6, -3.2, 0.0, 1.2, 1.0, -1.1]

BANDS = 8
LANES = 128
CLASSES = 3
WIDTH = 16
VMEM_BYTES = 8 * 2**20
ROOT = math.sqrt(10.0)
DECIBEL = math.log(10.0) / 10.0
NT = (((1,), (1,)), ((), ()))


def iota(shape, axis):
    return lax.broadcasted_iota(jnp.int32, shape, axis)


def hour_class(shape):
    hour = iota(shape, 0)
    day = (hour >= 7) & (hour < 19)
    evening = (hour >= 19) & (hour < 23)
    return jnp.where(day, 0, jnp.where(evening, 1, 2))


def band_terms(band, speed_kmh, log_ratio):
    shift = aweight_db[band] - 90.0
    rolling = jnp.exp(
        DECIBEL * (rolling_base[band] + shift) + (DECIBEL * rolling_slope[band]) * log_ratio
    )
    propel = jnp.exp(
        DECIBEL * (propel_base[band] + shift)
        + (DECIBEL * propel_slope[band] / 70.0) * (speed_kmh - 70.0)
    )
    return rolling, propel


def lane_pick(table, index):
    return jnp.take_along_axis(table, index, axis=1, mode="promise_in_bounds")


def turn(block, groups):
    shift = groups * WIDTH % LANES
    return pltpu.roll(block, shift, 1) if shift else block


def split2(value):
    high = value.astype(jnp.bfloat16)
    low = (value - high.astype(jnp.float32)).astype(jnp.bfloat16)
    return high, low


def source_kernel(copies, flow_hbm, speed_hbm, out_ref, flow_ref, speed_ref, sems):
    fetches = [
        pltpu.make_async_copy(flow_hbm, flow_ref, sems.at[0]),
        pltpu.make_async_copy(speed_hbm, speed_ref, sems.at[1]),
    ]
    for fetch in fetches:
        fetch.start()
    for fetch in fetches:
        fetch.wait()
    flow, speed = flow_ref[...], speed_ref[...]
    kind = hour_class(flow.shape)
    weight = jnp.where(kind == 0, 1.0, jnp.where(kind == 1, ROOT, 10.0))
    speed_kmh = 100.0 * speed
    log_ratio = jnp.log(speed_kmh / 70.0) * (1.0 / math.log(10.0))
    scale = weight * flow / speed_kmh
    row = iota((BANDS, LANES), 0)
    result = jnp.zeros((BANDS, LANES), jnp.float32)
    for band in range(BANDS):
        rolling, propel = band_terms(band, speed_kmh, log_ratio)
        total = jnp.sum(scale * (rolling + propel), axis=0, keepdims=True)
        result = jnp.where(row == band, total, result)
    for copy in range(copies):
        out_ref[copy * BANDS : (copy + 1) * BANDS] = result


def prepare_kernel(
    pairs_hbm, flow_hbm, speed_hbm, slot_hbm, relay_hbm, length_hbm, people_hbm, tile_hbm,
    table_ref, spread_ref, ints_ref, floats_ref, people_ref, tile_ref, pairs_ref, flow_ref, speed_ref, relay_ref, relay_scratch, sems,
):
    owners, blocks = relay_hbm.shape[0], slot_hbm.shape[0]
    index_ref, slot_ref = ints_ref.at[:owners], ints_ref.at[owners:]
    wide_ref, length_ref = floats_ref.at[:owners], floats_ref.at[owners:]
    moves = [
        (flow_hbm, flow_ref),
        (speed_hbm, speed_ref),
        (relay_hbm, relay_ref),
        (slot_hbm, slot_ref),
        (pairs_hbm, pairs_ref),
        (length_hbm, length_ref),
        (people_hbm, people_ref),
        (tile_hbm, tile_ref),
    ]
    fetches = [
        pltpu.make_async_copy(start, end, sems.at[k]) for k, (start, end) in enumerate(moves)
    ]
    for fetch in fetches:
        fetch.start()
    for fetch in fetches[:4]:
        fetch.wait()
    relay_scratch[...] = jnp.zeros(relay_scratch.shape, jnp.int32)
    relay_scratch[:, :WIDTH] = relay_ref[...]
    lane, row = iota((8, LANES), 1), iota((8, LANES), 0)
    for group in range(owners // 8):
        rows = slice(group * 8, group * 8 + 8)
        wide = lane_pick(relay_scratch[rows], lane % WIDTH)
        wide_ref[rows] = wide.astype(jnp.float32)
        picked = jnp.where(lane // WIDTH == row, jnp.maximum(wide, 0), 0)
        picked = jnp.sum(picked, axis=0, keepdims=True)
        index_ref[rows] = jnp.broadcast_to(picked, (8, LANES))
    flow, speed = flow_ref[...], speed_ref[...]
    speed_kmh = 100.0 * speed
    log_ratio = jnp.log(speed_kmh / 70.0) * (1.0 / math.log(10.0))
    per_flow = 1.0 / speed_kmh
    factor = flow * per_flow
    inverse = 1.0 / speed
    for band in range(BANDS):
        rolling, propel = band_terms(band, speed_kmh, log_ratio)
        table_ref[band] = per_flow * (rolling + propel)
        table_ref[BANDS + band] = factor * (
            rolling * (rolling_slope[band] / 10.0 - 1.0) * inverse
            + propel * (math.log(10.0) * propel_slope[band] / 7.0 - inverse)
        )
    slots = spread_ref.shape[0]
    for block in range(blocks):
        same = iota((slots, LANES), 0) == slot_ref[block : block + 1]
        spread_ref[:, block * LANES : (block + 1) * LANES] = jnp.where(
            same, 1.0, 0.0
        ).astype(jnp.bfloat16)
    for fetch in fetches[4:]:
        fetch.wait()


def forward_kernel(
    copies, pairs_ref, count_ref, link_ref, ints_ref, floats_ref, tile_ref, out_ref,
    seg_scratch, acc_scratch,
):
    owners = link_ref.shape[0] // BANDS
    groups = owners // 8
    index_ref, slot_ref, length_ref = ints_ref, ints_ref.at[owners:], floats_ref.at[owners:]
    lane = iota((BANDS, LANES), 1)
    tables = []
    for group in range(groups):
        index = index_ref[group * 8 : group * 8 + 8]
        table = jnp.zeros((BANDS, LANES), jnp.float32)
        for member in range(8):
            owner = group * 8 + member
            picked = lane_pick(link_ref[owner * BANDS : (owner + 1) * BANDS], index)
            table = jnp.where(lane // 16 == member, picked, table)
        tables.append(table)
    blocks = slot_ref.shape[0]
    for block in range(blocks):
        slot = jnp.broadcast_to(slot_ref[block : block + 1], (BANDS, LANES))
        value = lane_pick(tables[0], slot % LANES)
        for group in range(1, groups):
            value = jnp.where(slot // LANES == group, lane_pick(tables[group], slot % LANES), value)
        high, low = split2(value * length_ref[block : block + 1])
        seg_scratch[block] = jnp.concatenate([high, low], axis=0)
    acc_scratch[...] = jnp.zeros(acc_scratch.shape, jnp.float32)
    row = iota((2 * BANDS, LANES), 0) % BANDS

    def tile(step, carry):
        seg = seg_scratch[pairs_ref[0, step]]
        facade = pairs_ref[1, step]
        rows = jnp.concatenate(
            [jnp.where(row == band, seg, jnp.zeros_like(seg)) for band in range(BANDS)], axis=1
        )
        tiles = tile_ref[step].reshape(BANDS * LANES, LANES)
        acc_scratch[facade] += jnp.dot(rows, tiles, preferred_element_type=jnp.float32)
        return carry

    lax.fori_loop(0, count_ref[0, 0], tile, 0)
    facades = acc_scratch.shape[0]
    sums = [jnp.sum(acc_scratch[block], axis=0, keepdims=True) for block in range(facades)]
    result = jnp.concatenate(sums, axis=0)
    for copy in range(copies):
        out_ref[copy * facades : (copy + 1) * facades] = result


def backward_kernel(
    hours_weight, receivers, pairs_ref, count_ref, part_ref, people_ref, floats_ref,
    spread_ref, tile_ref, out_ref, grad_scratch, acc_scratch,
):
    facades = people_ref.shape[0]
    owners = out_ref.shape[0] // (receivers * BANDS)
    relay_ref, length_ref = floats_ref, floats_ref.at[owners:]
    sources = part_ref.shape[0] // facades
    total = part_ref[0:facades]
    for source in range(1, sources):
        total = total + part_ref[source * facades : (source + 1) * facades]
    total = total + 0.01 * hours_weight
    level = 60.0 + (10.0 / math.log(10.0)) * jnp.log(total / 24.0)
    people = people_ref[...].astype(jnp.float32)
    annoyed = people * (78.927 - 3.1162 * level + 0.0342 * level * level) / 100.0
    annoyed = jnp.sum(annoyed, keepdims=True)
    slope = people * (-3.1162 + 0.0684 * level) / 100.0 * (10.0 / math.log(10.0)) / total
    grads = [slope, slope * ROOT, slope * 10.0]
    pad = jnp.zeros((8, LANES), jnp.float32)
    for block in range(facades):
        rows = [jnp.broadcast_to(g[block : block + 1], (BANDS, LANES)) for g in grads]
        grad_scratch[block] = jnp.concatenate(rows + [pad], axis=0).astype(jnp.bfloat16)
    acc_scratch[...] = jnp.zeros(acc_scratch.shape, jnp.float32)
    row = iota((32, LANES), 0) % BANDS

    def tile(step, carry):
        block = pairs_ref[0, step]
        grad = grad_scratch[pairs_ref[1, step]]
        acc = acc_scratch[block]
        for band in range(BANDS):
            acc = acc + lax.dot_general(
                jnp.where(row == band, grad, jnp.zeros_like(grad)),
                tile_ref[step, band],
                NT,
                preferred_element_type=jnp.float32,
            )
        acc_scratch[block] = acc
        return carry

    lax.fori_loop(0, count_ref[0, 0], tile, 0)
    used = CLASSES * BANDS
    blocks = acc_scratch.shape[0]
    high, low = [], []
    for block in range(blocks):
        value = acc_scratch[block][:used] * length_ref[block : block + 1]
        high_part = value.astype(jnp.bfloat16).astype(jnp.float32)
        high.append(high_part)
        low.append(value - high_part)
    rows = jnp.concatenate(
        [jnp.concatenate(high, axis=1), jnp.concatenate(low, axis=1)], axis=0
    ).astype(jnp.bfloat16)
    slots = lax.dot_general(rows, spread_ref[...], NT, preferred_element_type=jnp.float32)
    slots = slots[:used] + slots[used:]
    place = iota((BANDS, LANES), 1) // WIDTH
    for group in range(owners // 8):
        lanes = slice(group * LANES, (group + 1) * LANES)
        parts = [
            turn(slots[kind * BANDS : (kind + 1) * BANDS, lanes], kind) for kind in range(CLASSES)
        ]
        for member in range(8):
            owner = group * 8 + member
            block = jnp.where(
                place == (member + CLASSES) % 8, relay_ref[owner : owner + 1], annoyed
            )
            for kind in range(CLASSES):
                block = jnp.where(place == (member + kind) % 8, parts[kind], block)
            block = turn(block, -member)
            for receiver in range(receivers):
                first = (receiver * owners + owner) * BANDS
                out_ref[first : first + BANDS] = block


def finish_kernel(receivers, in_ref, table_ref, flow_out, speed_out, count_out):
    owners = in_ref.shape[0] // (receivers * BANDS)
    place = iota((BANDS, LANES), 1) // WIDTH
    used = CLASSES * BANDS
    links = jnp.zeros((2 * used, LANES), jnp.float32)
    for group in range(owners // 8):
        parts = [jnp.zeros((BANDS, LANES), jnp.float32)] * (CLASSES + 1)
        for member in range(8):
            owner = group * 8 + member
            first = in_ref[owner * BANDS : (owner + 1) * BANDS]
            total = first
            for receiver in range(1, receivers):
                start = (receiver * owners + owner) * BANDS
                total = total + in_ref[start : start + BANDS]
            if owner == 0:
                count_out[...] = jnp.broadcast_to(total[0:1, LANES - 1 :], (1, LANES))
            total = turn(jnp.where(place == CLASSES, first, total), member)
            for kind in range(CLASSES + 1):
                parts[kind] = jnp.where(place == (member + kind) % 8, total, parts[kind])
        parts = [turn(part, -kind) for kind, part in enumerate(parts)]
        value = jnp.concatenate(parts[:CLASSES], axis=0)
        high = value.astype(jnp.bfloat16).astype(jnp.float32)
        rows = jnp.concatenate([high, value - high], axis=0).astype(jnp.bfloat16)
        relay = parts[CLASSES][0:1].astype(jnp.int32)
        spread = jnp.where(iota((LANES, LANES), 0) == relay, 1.0, 0.0).astype(jnp.bfloat16)
        links = links + lax.dot_general(rows, spread, NT, preferred_element_type=jnp.float32)
    links = links[:used] + links[used:]
    kind = hour_class(flow_out.shape)
    flow_sum = jnp.zeros(flow_out.shape, jnp.float32)
    speed_sum = jnp.zeros(flow_out.shape, jnp.float32)
    for band in range(BANDS):
        day, evening, night = [
            links[k * BANDS + band : k * BANDS + band + 1] for k in range(CLASSES)
        ]
        back = jnp.where(kind == 0, day, jnp.where(kind == 1, evening, night))
        flow_sum = flow_sum + back * table_ref[band]
        speed_sum = speed_sum + back * table_ref[BANDS + band]
    flow_out[...] = flow_sum
    speed_out[...] = speed_sum


def call(kernel, name, outs, args, scratch=()):
    space = {"smem": pltpu.SMEM, "vmem": pltpu.VMEM, "hbm": pltpu.HBM}
    return pl.pallas_call(
        kernel,
        out_shape=[
            space[place](shape, dtype) if place else jax.ShapeDtypeStruct(shape, dtype)
            for shape, dtype, place in outs
        ],
        in_specs=[pl.BlockSpec(memory_space=space[place or "smem"]) for _, place in args],
        out_specs=[pl.BlockSpec(memory_space=space[place or "vmem"]) for _, _, place in outs],
        scratch_shapes=list(scratch),
        compiler_params=pltpu.CompilerParams(vmem_limit_bytes=VMEM_BYTES),
        name=name,
    )(
        *[
            pltpu.with_memory_space_constraint(array, space[place]) if place else array
            for array, place in args
        ]
    )


def shards(
    flows, speeds, seg_length, relay_list, seg_slot, tile_pairs, tile_count, attenuation, dwellings
):
    sources, receivers = lax.axis_size("src"), lax.axis_size("rcv")
    hours = flows.shape[0]
    slots = sources * WIDTH
    f32, i32, bf16 = jnp.float32, jnp.int32, jnp.bfloat16
    blocks, facades = seg_slot.shape[0] // LANES, dwellings.shape[0] // LANES
    hours_weight = sum(
        1.0 if 7 <= h < 19 else (ROOT if 19 <= h < 23 else 10.0) for h in range(hours)
    )

    def vmem(shape, dtype):
        return (shape, dtype, "vmem")

    (power,) = call(
        functools.partial(source_kernel, sources),
        "source",
        [vmem((sources * BANDS, LANES), f32)],
        [(flows, "hbm"), (speeds, "hbm")],
        [
            pltpu.VMEM((hours, LANES), f32),
            pltpu.VMEM((hours, LANES), f32),
            pltpu.SemaphoreType.DMA((2,)),
        ],
    )
    power = lax.all_to_all(power, "src", 0, 0, tiled=True)
    tables, spread, ints, floats, people, tiles, pairs = call(
        prepare_kernel,
        "prepare",
        [
            vmem((2 * BANDS, hours, LANES), f32),
            vmem((slots, blocks * LANES), bf16),
            vmem((sources + blocks, LANES), i32),
            vmem((sources + blocks, LANES), f32),
            vmem((facades, LANES), i32),
            vmem(attenuation.shape[2:], bf16),
            (tile_pairs.shape[2:], i32, "smem"),
        ],
        [
            (array, "hbm")
            for array in (
                tile_pairs[0, 0],
                flows,
                speeds,
                seg_slot.reshape(blocks, LANES),
                relay_list[0],
                seg_length.reshape(blocks, LANES),
                dwellings.reshape(facades, LANES),
                attenuation[0, 0],
            )
        ],
        [
            pltpu.VMEM((hours, LANES), f32),
            pltpu.VMEM((hours, LANES), f32),
            pltpu.VMEM((sources, WIDTH), i32),
            pltpu.VMEM((sources, LANES), i32),
            pltpu.SemaphoreType.DMA((8,)),
        ],
    )
    here = [(pairs, "smem"), (tile_count, "")]
    (part,) = call(
        functools.partial(forward_kernel, sources),
        "forward",
        [vmem((sources * facades, LANES), f32)],
        here + [(array, "vmem") for array in (power, ints, floats, tiles)],
        [
            pltpu.VMEM((blocks, 2 * BANDS, LANES), bf16),
            pltpu.VMEM((facades, 2 * BANDS, LANES), f32),
        ],
    )
    part = lax.all_to_all(part, "src", 0, 0, tiled=True)
    (back,) = call(
        functools.partial(backward_kernel, hours_weight, receivers),
        "backward",
        [vmem((receivers * sources * BANDS, LANES), f32)],
        here + [(array, "vmem") for array in (part, people, floats, spread, tiles)],
        [
            pltpu.VMEM((facades, 32, LANES), bf16),
            pltpu.VMEM((blocks, 32, LANES), f32),
        ],
    )
    back = lax.all_to_all(back, ("rcv", "src"), 0, 0, tiled=True)
    grad_flows, grad_speeds, annoyed = call(
        functools.partial(finish_kernel, receivers),
        "finish",
        [((hours, LANES), f32, ""), ((hours, LANES), f32, ""), ((1, LANES), f32, "")],
        [(array, "vmem") for array in (back, tables)],
    )
    return grad_flows, grad_speeds, annoyed[0, 0]


def solution(mesh):
    in_specs = (
        P(None, "src"),
        P(None, "src"),
        P("src"),
        P("src", None, None),
        P("src"),
        P("src", "rcv", None, None),
        P("src", "rcv"),
        P("src", "rcv", None, None, None, None),
        P("rcv"),
    )
    out_specs = (P(None, "src"), P(None, "src"), P())
    return jax.shard_map(shards, mesh=mesh, in_specs=in_specs, out_specs=out_specs, check_vma=False)
```

```python
import functools
import math

import jax
import jax.numpy as jnp
from jax import lax
from jax.experimental import pallas as pl
from jax.experimental.pallas import tpu as pltpu
from jax.sharding import PartitionSpec as P

rolling_base = [79.7, 85.7, 84.5, 90.2, 97.3, 93.9, 84.1, 74.3]
rolling_slope = [30.0, 41.5, 38.9, 25.7, 32.5, 37.2, 39.0, 40.0]
propel_base = [94.5, 89.2, 88.0, 85.9, 84.2, 86.9, 83.3, 76.1]
propel_slope = [-1.3, 7.2, 7.7, 8.0, 8.0, 8.0, 8.0, 8.0]
aweight_db = [-26.2, -16.1, -8.6, -3.2, 0.0, 1.2, 1.0, -1.1]

BANDS = 8
LANES = 128
CLASSES = 3
WIDTH = 16
VMEM_BYTES = 8 * 2**20
ROWS = 4
TOGETHER = 6
ROOT = math.sqrt(10.0)
DECIBEL = math.log(10.0) / 10.0
NT = (((1,), (1,)), ((), ()))


def iota(shape, axis):
    return lax.broadcasted_iota(jnp.int32, shape, axis)


def hour_class(shape):
    hour = iota(shape, 0)
    day = (hour >= 7) & (hour < 19)
    evening = (hour >= 19) & (hour < 23)
    return jnp.where(day, 0, jnp.where(evening, 1, 2))


def band_terms(band, speed_kmh, log_ratio):
    shift = aweight_db[band] - 90.0
    rolling = jnp.exp(
        DECIBEL * (rolling_base[band] + shift) + (DECIBEL * rolling_slope[band]) * log_ratio
    )
    propel = jnp.exp(
        DECIBEL * (propel_base[band] + shift)
        + (DECIBEL * propel_slope[band] / 70.0) * (speed_kmh - 70.0)
    )
    return rolling, propel


def lane_pick(table, index):
    return jnp.take_along_axis(table, index, axis=1, mode="promise_in_bounds")


def swap_groups(block):
    row, lane = iota((8, LANES), 0), iota((8, LANES), 1)
    block = lane_pick(block, (lane + LANES - WIDTH * row) % LANES)
    block = jnp.take_along_axis(
        block, (lane // WIDTH + 8 - row) % 8, axis=0, mode="promise_in_bounds"
    )
    return lane_pick(block, (lane + WIDTH * row) % LANES)


def each_tile(pairs_ref, count, read, multiply, write, acc_ref):
    def step(turn, carry):
        added = []
        for place in range(TOGETHER):
            number = turn * TOGETHER + place
            tile = jnp.minimum(number, count - 1)
            value = read(tile)
            value = jnp.where(number < count, value, jnp.zeros_like(value))
            added.append((write(tile), multiply(value, tile)))
        for block, value in added:
            acc_ref[block] += value
        return carry

    lax.fori_loop(0, (count + TOGETHER - 1) // TOGETHER, step, 0)


def only_band(value, band):
    row = iota(value.shape, 0) % BANDS
    return jnp.where(row == band, value, jnp.zeros_like(value))


def split2(value):
    high = value.astype(jnp.bfloat16)
    low = (value - high.astype(jnp.float32)).astype(jnp.bfloat16)
    return high, low


def source_kernel(copies, flow_hbm, speed_hbm, out_ref, flow_ref, speed_ref, sems):
    fetches = [
        pltpu.make_async_copy(flow_hbm, flow_ref, sems.at[0]),
        pltpu.make_async_copy(speed_hbm, speed_ref, sems.at[1]),
    ]
    for fetch in fetches:
        fetch.start()
    for fetch in fetches:
        fetch.wait()
    flow, speed = flow_ref[...], speed_ref[...]
    kind = hour_class(flow.shape)
    weight = jnp.where(kind == 0, 1.0, jnp.where(kind == 1, ROOT, 10.0))
    speed_kmh = 100.0 * speed
    log_ratio = jnp.log(speed_kmh / 70.0) * (1.0 / math.log(10.0))
    scale = weight * flow / speed_kmh
    row = iota((BANDS, LANES), 0)
    result = jnp.zeros((BANDS, LANES), jnp.float32)
    for band in range(BANDS):
        rolling, propel = band_terms(band, speed_kmh, log_ratio)
        total = jnp.sum(scale * (rolling + propel), axis=0, keepdims=True)
        result = jnp.where(row == band, total, result)
    for copy in range(copies):
        out_ref[copy * BANDS : (copy + 1) * BANDS] = result


def prepare_kernel(
    pairs_hbm, flow_hbm, speed_hbm, slot_hbm, relay_hbm, length_hbm, people_hbm, tile_hbm,
    table_ref, spread_ref, ints_ref, floats_ref, people_ref, tile_ref, pairs_ref, flow_ref, speed_ref, relay_ref, relay_scratch, sems,
):
    owners, blocks = relay_hbm.shape[0], slot_hbm.shape[0]
    index_ref, slot_ref = ints_ref.at[:owners], ints_ref.at[owners:]
    wide_ref, length_ref = floats_ref.at[:owners], floats_ref.at[owners:]
    moves = [
        (flow_hbm, flow_ref),
        (speed_hbm, speed_ref),
        (relay_hbm, relay_ref),
        (slot_hbm, slot_ref),
        (pairs_hbm, pairs_ref),
        (length_hbm, length_ref),
        (people_hbm, people_ref),
        (tile_hbm, tile_ref),
    ]
    fetches = [
        pltpu.make_async_copy(start, end, sems.at[k]) for k, (start, end) in enumerate(moves)
    ]
    for fetch in fetches:
        fetch.start()
    for fetch in fetches[:4]:
        fetch.wait()
    relay_scratch[...] = jnp.zeros(relay_scratch.shape, jnp.int32)
    relay_scratch[:, :WIDTH] = relay_ref[...]
    lane, row = iota((8, LANES), 1), iota((8, LANES), 0)
    for group in range(owners // 8):
        rows = slice(group * 8, group * 8 + 8)
        wide = lane_pick(relay_scratch[rows], lane % WIDTH)
        wide_ref[rows] = wide.astype(jnp.float32)
        picked = jnp.where(lane // WIDTH == row, jnp.maximum(wide, 0), 0)
        picked = jnp.sum(picked, axis=0, keepdims=True)
        index_ref[rows] = jnp.broadcast_to(picked, (8, LANES))
    flow, speed = flow_ref[...], speed_ref[...]
    speed_kmh = 100.0 * speed
    log_ratio = jnp.log(speed_kmh / 70.0) * (1.0 / math.log(10.0))
    per_flow = 1.0 / speed_kmh
    factor = flow * per_flow
    inverse = 1.0 / speed
    for band in range(BANDS):
        rolling, propel = band_terms(band, speed_kmh, log_ratio)
        table_ref[band] = per_flow * (rolling + propel)
        table_ref[BANDS + band] = factor * (
            rolling * (rolling_slope[band] / 10.0 - 1.0) * inverse
            + propel * (math.log(10.0) * propel_slope[band] / 7.0 - inverse)
        )
    slots = spread_ref.shape[1]
    for block in range(blocks):
        same = iota((slots, LANES), 0) == slot_ref[block : block + 1]
        spread_ref[block * LANES : (block + 1) * LANES] = (
            jnp.where(same, 1.0, 0.0).T.astype(jnp.bfloat16)
        )
    for fetch in fetches[4:]:
        fetch.wait()


def turn_kernel(count_ref, tile_ref, part_ref, out_ref):
    def step(tile, carry):
        for band in range(BANDS):
            out_ref[tile, band] = tile_ref[tile, band].T
        return carry

    lax.fori_loop(0, count_ref[0, 0], step, 0)


def forward_kernel(own_blocks, copies, pairs_ref, count_ref, ints_ref, floats_ref, tile_ref, *refs):
    link_refs, (out_ref, seg_scratch, acc_scratch) = refs[:-3], refs[-3:]
    each = link_refs[0].shape[0] // BANDS
    owners = each * len(link_refs)
    groups = owners // 8
    index_ref, slot_ref, length_ref = ints_ref, ints_ref.at[owners:], floats_ref.at[owners:]
    place = iota((BANDS, LANES), 1) // WIDTH
    tables = []
    for group in range(groups):
        index = index_ref[group * 8 : group * 8 + 8]
        table = jnp.zeros((BANDS, LANES), jnp.float32)
        for member in range(8):
            block = group * 8 + member
            rows = slice(block % each * BANDS, (block % each + 1) * BANDS)
            picked = lane_pick(link_refs[block // each][rows], index)
            if own_blocks:
                member = lax.axis_index("src") ^ member
            table = jnp.where(place == member, picked, table)
        tables.append(table)
    blocks = slot_ref.shape[0]
    for block in range(blocks):
        slot = jnp.broadcast_to(slot_ref[block : block + 1], (BANDS, LANES))
        value = lane_pick(tables[0], slot % LANES)
        for group in range(1, groups):
            value = jnp.where(slot // LANES == group, lane_pick(tables[group], slot % LANES), value)
        high, low = split2(value * length_ref[block : block + 1])
        seg_scratch[block] = jnp.concatenate([high, low], axis=0)
    acc_scratch[...] = jnp.zeros(acc_scratch.shape, jnp.float32)

    def multiply(seg, tile):
        rows = jnp.concatenate([only_band(seg, band) for band in range(BANDS)], axis=1)
        tiles = tile_ref[tile].reshape(BANDS * LANES, LANES)
        return jnp.dot(rows, tiles, preferred_element_type=jnp.float32)

    each_tile(
        pairs_ref,
        count_ref[0, 0],
        lambda tile: seg_scratch[pairs_ref[0, tile]],
        multiply,
        lambda tile: pairs_ref[1, tile],
        acc_scratch,
    )
    facades = acc_scratch.shape[0]
    sums = [jnp.sum(acc_scratch[block], axis=0, keepdims=True) for block in range(facades)]
    result = jnp.concatenate(sums, axis=0)
    for copy in range(copies):
        out_ref[copy * facades : (copy + 1) * facades] = result


def backward_kernel(
    hours_weight, receivers, pairs_ref, count_ref, people_ref, floats_ref, spread_ref, tile_ref, *refs
):
    part_refs, (out_ref, grad_scratch, acc_scratch) = refs[:-3], refs[-3:]
    facades = people_ref.shape[0]
    owners = out_ref.shape[0] // (receivers * ROWS)
    relay_ref, length_ref = floats_ref, floats_ref.at[owners:]
    parts = [
        ref[first : first + facades]
        for ref in part_refs
        for first in range(0, ref.shape[0], facades)
    ]
    while len(parts) > 1:
        parts = [sum(parts[k + 1 : k + 2], parts[k]) for k in range(0, len(parts), 2)]
    (total,) = parts
    total = total + 0.01 * hours_weight
    level = 60.0 + (10.0 / math.log(10.0)) * jnp.log(total / 24.0)
    people = people_ref[...].astype(jnp.float32)
    annoyed = people * (78.927 - 3.1162 * level + 0.0342 * level * level) / 100.0
    annoyed = jnp.sum(annoyed, keepdims=True)
    slope = people * (-3.1162 + 0.0684 * level) / 100.0 * (10.0 / math.log(10.0)) / total
    grads = [slope, slope * ROOT, slope * 10.0]
    pad = jnp.zeros((8, LANES), jnp.float32)
    for block in range(facades):
        rows = [jnp.broadcast_to(g[block : block + 1], (BANDS, LANES)) for g in grads]
        grad_scratch[block] = jnp.concatenate(rows + [pad], axis=0).astype(jnp.bfloat16)
    acc_scratch[...] = jnp.zeros(acc_scratch.shape, jnp.float32)

    def multiply(grad, tile):
        rows = jnp.concatenate([only_band(grad, band) for band in range(BANDS)], axis=1)
        tiles = tile_ref[tile].reshape(BANDS * LANES, LANES)
        return jnp.dot(rows, tiles, preferred_element_type=jnp.float32)

    each_tile(
        pairs_ref,
        count_ref[0, 0],
        lambda tile: grad_scratch[pairs_ref[1, tile]],
        multiply,
        lambda tile: pairs_ref[0, tile],
        acc_scratch,
    )
    used = CLASSES * BANDS
    blocks = acc_scratch.shape[0]
    high, low = [], []
    for block in range(blocks):
        value = acc_scratch[block][:used] * length_ref[block : block + 1]
        high_part = value.astype(jnp.bfloat16).astype(jnp.float32)
        high.append(high_part)
        low.append(value - high_part)
    rows = jnp.concatenate(
        [jnp.concatenate(high, axis=1), jnp.concatenate(low, axis=1)], axis=0
    ).astype(jnp.bfloat16)
    slots = jnp.dot(rows, spread_ref[...], preferred_element_type=jnp.float32)
    slots = slots[:used] + slots[used:]
    place = iota((8, LANES), 1) // WIDTH
    for group in range(owners // 8):
        lanes = slice(group * LANES, (group + 1) * LANES)
        rows = [
            swap_groups(slots[kind * BANDS : (kind + 1) * BANDS, lanes])
            for kind in range(CLASSES)
        ]
        rows.append(jnp.where(place == 0, relay_ref[group * 8 : group * 8 + 8], annoyed))
        for receiver in range(receivers):
            first = (receiver * owners + group * 8) * ROWS
            for kind in range(ROWS):
                out_ref[pl.ds(first + kind, 8, stride=ROWS), :] = rows[kind]


def finish_kernel(receivers, in_ref, table_ref, flow_out, speed_out, count_out):
    owners = in_ref.shape[0] // (receivers * ROWS)
    place, row = iota((8, LANES), 1) // WIDTH, iota((8, LANES), 0)
    used = CLASSES * BANDS
    links = jnp.zeros((2 * used, LANES), jnp.float32)
    for group in range(owners // 8):
        parts = []
        for kind in range(ROWS):
            rows = [
                in_ref[pl.ds((receiver * owners + group * 8) * ROWS + kind, 8, stride=ROWS), :]
                for receiver in range(receivers)
            ]
            total = sum(rows[1:], rows[0])
            parts.append(swap_groups(total) if kind < CLASSES else rows[0])
        if group == 0:
            count_out[...] = jnp.broadcast_to(total[0:1, LANES - 1 :], (1, LANES))
        value = jnp.concatenate(parts[:CLASSES], axis=0)
        high = value.astype(jnp.bfloat16).astype(jnp.float32)
        rows = jnp.concatenate([high, value - high], axis=0).astype(jnp.bfloat16)
        relay = lane_pick(parts[CLASSES], iota((8, LANES), 1) % WIDTH)
        relay = jnp.sum(jnp.where(place == row, relay, 0.0), axis=0, keepdims=True)
        relay = relay.astype(jnp.int32)
        spread = jnp.where(iota((LANES, LANES), 0) == relay, 1.0, 0.0).astype(jnp.bfloat16)
        links = links + lax.dot_general(rows, spread, NT, preferred_element_type=jnp.float32)
    links = links[:used] + links[used:]
    kind = hour_class(flow_out.shape)
    flow_sum = jnp.zeros(flow_out.shape, jnp.float32)
    speed_sum = jnp.zeros(flow_out.shape, jnp.float32)
    for band in range(BANDS):
        day, evening, night = [
            links[k * BANDS + band : k * BANDS + band + 1] for k in range(CLASSES)
        ]
        back = jnp.where(kind == 0, day, jnp.where(kind == 1, evening, night))
        flow_sum = flow_sum + back * table_ref[band]
        speed_sum = speed_sum + back * table_ref[BANDS + band]
    flow_out[...] = flow_sum
    speed_out[...] = speed_sum


def call(kernel, name, outs, args, scratch=()):
    space = {"smem": pltpu.SMEM, "vmem": pltpu.VMEM, "hbm": pltpu.HBM}
    return pl.pallas_call(
        kernel,
        out_shape=[
            space[place](shape, dtype) if place else jax.ShapeDtypeStruct(shape, dtype)
            for shape, dtype, place in outs
        ],
        in_specs=[pl.BlockSpec(memory_space=space[place or "smem"]) for _, place in args],
        out_specs=[pl.BlockSpec(memory_space=space[place or "vmem"]) for _, _, place in outs],
        scratch_shapes=list(scratch),
        compiler_params=pltpu.CompilerParams(vmem_limit_bytes=VMEM_BYTES),
        name=name,
    )(
        *[
            pltpu.with_memory_space_constraint(array, space[place]) if place else array
            for array, place in args
        ]
    )


def pair(array, distance):
    sources = lax.axis_size("src")
    return lax.ppermute(array, "src", [(k, k ^ distance) for k in range(sources)])


def shards(
    flows, speeds, seg_length, relay_list, seg_slot, tile_pairs, tile_count, attenuation, dwellings
):
    sources, receivers = lax.axis_size("src"), lax.axis_size("rcv")
    hours = flows.shape[0]
    slots = sources * WIDTH
    f32, i32, bf16 = jnp.float32, jnp.int32, jnp.bfloat16
    blocks, facades = seg_slot.shape[0] // LANES, dwellings.shape[0] // LANES
    hours_weight = sum(
        1.0 if 7 <= h < 19 else (ROOT if 19 <= h < 23 else 10.0) for h in range(hours)
    )

    def vmem(shape, dtype):
        return (shape, dtype, "vmem")

    pairwise = sources == 8
    copies = 1 if pairwise else sources
    (power,) = call(
        functools.partial(source_kernel, copies),
        "source",
        [vmem((copies * BANDS, LANES), f32)],
        [(flows, "hbm"), (speeds, "hbm")],
        [
            pltpu.VMEM((hours, LANES), f32),
            pltpu.VMEM((hours, LANES), f32),
            pltpu.SemaphoreType.DMA((2,)),
        ],
    )
    if pairwise:
        power = jnp.concatenate([power, pair(power, 1)], axis=0)
        powers = [power] + [pair(power, distance) for distance in (2, 4, 6)]
    else:
        powers = [lax.all_to_all(power, "src", 0, 0, tiled=True)]
    tables, spread, ints, floats, people, tiles, pairs = call(
        prepare_kernel,
        "prepare",
        [
            vmem((2 * BANDS, hours, LANES), f32),
            vmem((blocks * LANES, slots), bf16),
            vmem((sources + blocks, LANES), i32),
            vmem((sources + blocks, LANES), f32),
            vmem((facades, LANES), i32),
            vmem(attenuation.shape[2:], bf16),
            (tile_pairs.shape[2:], i32, "smem"),
        ],
        [
            (array, "hbm")
            for array in (
                tile_pairs[0, 0],
                flows,
                speeds,
                seg_slot.reshape(blocks, LANES),
                relay_list[0],
                seg_length.reshape(blocks, LANES),
                dwellings.reshape(facades, LANES),
                attenuation[0, 0],
            )
        ],
        [
            pltpu.VMEM((hours, LANES), f32),
            pltpu.VMEM((hours, LANES), f32),
            pltpu.VMEM((sources, WIDTH), i32),
            pltpu.VMEM((sources, LANES), i32),
            pltpu.SemaphoreType.DMA((8,)),
        ],
    )
    here = [(pairs, "smem"), (tile_count, "")]
    (part,) = call(
        functools.partial(forward_kernel, pairwise, copies),
        "forward",
        [vmem((copies * facades, LANES), f32)],
        here + [(array, "vmem") for array in (ints, floats, tiles, *powers)],
        [
            pltpu.VMEM((blocks, 2 * BANDS, LANES), bf16),
            pltpu.VMEM((facades, 2 * BANDS, LANES), f32),
        ],
    )
    if pairwise:
        total = part + pair(part, 1)
        parts = [total] + [pair(total, distance) for distance in (2, 4, 6)]
    else:
        parts = [lax.all_to_all(part, "src", 0, 0, tiled=True)]
    (turned,) = call(
        turn_kernel,
        "turn",
        [vmem(attenuation.shape[2:], bf16)],
        [(tile_count, ""), (tiles, "vmem"), (part, "vmem")],
    )
    (back,) = call(
        functools.partial(backward_kernel, hours_weight, receivers),
        "backward",
        [vmem((receivers * sources * ROWS, LANES), f32)],
        here + [(array, "vmem") for array in (people, floats, spread, turned, *parts)],
        [
            pltpu.VMEM((facades, 32, LANES), bf16),
            pltpu.VMEM((blocks, 32, LANES), f32),
        ],
    )
    back = back.reshape(receivers * sources, ROWS, LANES)
    back = lax.all_to_all(back, ("rcv", "src"), 0, 0, tiled=True)
    back = back.reshape(receivers * sources * ROWS, LANES)
    grad_flows, grad_speeds, annoyed = call(
        functools.partial(finish_kernel, receivers),
        "finish",
        [((hours, LANES), f32, ""), ((hours, LANES), f32, ""), ((1, LANES), f32, "")],
        [(array, "vmem") for array in (back, tables)],
    )
    return grad_flows, grad_speeds, annoyed[0, 0]


def solution(mesh):
    in_specs = (
        P(None, "src"),
        P(None, "src"),
        P("src"),
        P("src", None, None),
        P("src"),
        P("src", "rcv", None, None),
        P("src", "rcv"),
        P("src", "rcv", None, None, None, None),
        P("rcv"),
    )
    out_specs = (P(None, "src"), P(None, "src"), P())
    return jax.shard_map(shards, mesh=mesh, in_specs=in_specs, out_specs=out_specs, check_vma=False)
```

```python
import functools
import math

import jax
import jax.numpy as jnp
from jax import lax
from jax.experimental import pallas as pl
from jax.experimental.pallas import tpu as pltpu
from jax.sharding import PartitionSpec as P

rolling_base = [79.7, 85.7, 84.5, 90.2, 97.3, 93.9, 84.1, 74.3]
rolling_slope = [30.0, 41.5, 38.9, 25.7, 32.5, 37.2, 39.0, 40.0]
propel_base = [94.5, 89.2, 88.0, 85.9, 84.2, 86.9, 83.3, 76.1]
propel_slope = [-1.3, 7.2, 7.7, 8.0, 8.0, 8.0, 8.0, 8.0]
aweight_db = [-26.2, -16.1, -8.6, -3.2, 0.0, 1.2, 1.0, -1.1]

BANDS = 8
LANES = 128
CLASSES = 3
WIDTH = 16
VMEM_BYTES = 8 * 2**20
ROWS = 4
TOGETHER = 6
ROOT = math.sqrt(10.0)
DECIBEL = math.log(10.0) / 10.0
NT = (((1,), (1,)), ((), ()))


def iota(shape, axis):
    return lax.broadcasted_iota(jnp.int32, shape, axis)


def hour_class(shape):
    hour = iota(shape, 0)
    day = (hour >= 7) & (hour < 19)
    evening = (hour >= 19) & (hour < 23)
    return jnp.where(day, 0, jnp.where(evening, 1, 2))


def band_terms(band, speed_kmh, log_ratio):
    shift = aweight_db[band] - 90.0
    rolling = jnp.exp(
        DECIBEL * (rolling_base[band] + shift) + (DECIBEL * rolling_slope[band]) * log_ratio
    )
    propel = jnp.exp(
        DECIBEL * (propel_base[band] + shift)
        + (DECIBEL * propel_slope[band] / 70.0) * (speed_kmh - 70.0)
    )
    return rolling, propel


def lane_pick(table, index):
    return jnp.take_along_axis(table, index, axis=1, mode="promise_in_bounds")


def swap_groups(block):
    row, lane = iota((8, LANES), 0), iota((8, LANES), 1)
    block = lane_pick(block, (lane + LANES - WIDTH * row) % LANES)
    block = jnp.take_along_axis(
        block, (lane // WIDTH + 8 - row) % 8, axis=0, mode="promise_in_bounds"
    )
    return lane_pick(block, (lane + WIDTH * row) % LANES)


def each_tile(pairs_ref, count, read, multiply, write, acc_ref):
    def step(turn, carry):
        added = []
        for place in range(TOGETHER):
            number = turn * TOGETHER + place
            tile = jnp.minimum(number, count - 1)
            value = read(tile)
            value = jnp.where(number < count, value, jnp.zeros_like(value))
            added.append((write(tile), multiply(value, tile)))
        for block, value in added:
            acc_ref[block] += value
        return carry

    lax.fori_loop(0, (count + TOGETHER - 1) // TOGETHER, step, 0)


def only_band(value, band):
    row = iota(value.shape, 0) % BANDS
    return jnp.where(row == band, value, jnp.zeros_like(value))


def split2(value):
    high = value.astype(jnp.bfloat16)
    low = (value - high.astype(jnp.float32)).astype(jnp.bfloat16)
    return high, low


def source_kernel(copies, flow_hbm, speed_hbm, out_ref, flow_ref, speed_ref, sems):
    fetches = [
        pltpu.make_async_copy(flow_hbm, flow_ref, sems.at[0]),
        pltpu.make_async_copy(speed_hbm, speed_ref, sems.at[1]),
    ]
    for fetch in fetches:
        fetch.start()
    for fetch in fetches:
        fetch.wait()
    flow, speed = flow_ref[...], speed_ref[...]
    kind = hour_class(flow.shape)
    weight = jnp.where(kind == 0, 1.0, jnp.where(kind == 1, ROOT, 10.0))
    speed_kmh = 100.0 * speed
    log_ratio = jnp.log(speed_kmh / 70.0) * (1.0 / math.log(10.0))
    scale = weight * flow / speed_kmh
    row = iota((BANDS, LANES), 0)
    result = jnp.zeros((BANDS, LANES), jnp.float32)
    for band in range(BANDS):
        rolling, propel = band_terms(band, speed_kmh, log_ratio)
        total = jnp.sum(scale * (rolling + propel), axis=0, keepdims=True)
        result = jnp.where(row == band, total, result)
    for copy in range(copies):
        out_ref[copy * BANDS : (copy + 1) * BANDS] = result


def prepare_kernel(
    pairs_hbm, flow_hbm, speed_hbm, slot_hbm, relay_hbm, length_hbm, people_hbm, tile_hbm,
    table_ref, spread_ref, ints_ref, floats_ref, people_ref, tile_ref, pairs_ref, flow_ref, speed_ref, relay_ref, relay_scratch, sems,
):
    owners, blocks = relay_hbm.shape[0], slot_hbm.shape[0]
    index_ref, slot_ref = ints_ref.at[:owners], ints_ref.at[owners:]
    wide_ref, length_ref = floats_ref.at[:owners], floats_ref.at[owners:]
    moves = [
        (flow_hbm, flow_ref),
        (speed_hbm, speed_ref),
        (relay_hbm, relay_ref),
        (slot_hbm, slot_ref),
        (pairs_hbm, pairs_ref),
        (length_hbm, length_ref),
        (people_hbm, people_ref),
        (tile_hbm, tile_ref),
    ]
    fetches = [
        pltpu.make_async_copy(start, end, sems.at[k]) for k, (start, end) in enumerate(moves)
    ]
    for fetch in fetches:
        fetch.start()
    for fetch in fetches[:4]:
        fetch.wait()
    relay_scratch[...] = jnp.zeros(relay_scratch.shape, jnp.int32)
    relay_scratch[:, :WIDTH] = relay_ref[...]
    lane, row = iota((8, LANES), 1), iota((8, LANES), 0)
    for group in range(owners // 8):
        rows = slice(group * 8, group * 8 + 8)
        wide = lane_pick(relay_scratch[rows], lane % WIDTH)
        wide_ref[rows] = wide.astype(jnp.float32)
        picked = jnp.where(lane // WIDTH == row, jnp.maximum(wide, 0), 0)
        picked = jnp.sum(picked, axis=0, keepdims=True)
        index_ref[rows] = jnp.broadcast_to(picked, (8, LANES))
    flow, speed = flow_ref[...], speed_ref[...]
    speed_kmh = 100.0 * speed
    log_ratio = jnp.log(speed_kmh / 70.0) * (1.0 / math.log(10.0))
    per_flow = 1.0 / speed_kmh
    factor = flow * per_flow
    inverse = 1.0 / speed
    for band in range(BANDS):
        rolling, propel = band_terms(band, speed_kmh, log_ratio)
        table_ref[band] = per_flow * (rolling + propel)
        table_ref[BANDS + band] = factor * (
            rolling * (rolling_slope[band] / 10.0 - 1.0) * inverse
            + propel * (math.log(10.0) * propel_slope[band] / 7.0 - inverse)
        )
    slots = spread_ref.shape[1]
    for block in range(blocks):
        same = iota((slots, LANES), 0) == slot_ref[block : block + 1]
        spread_ref[block * LANES : (block + 1) * LANES] = (
            jnp.where(same, 1.0, 0.0).T.astype(jnp.bfloat16)
        )
    for fetch in fetches[4:]:
        fetch.wait()


def turn_kernel(count_ref, tile_ref, part_ref, out_ref):
    def step(tile, carry):
        for band in range(BANDS):
            out_ref[tile, band] = tile_ref[tile, band].T
        return carry

    lax.fori_loop(0, count_ref[0, 0], step, 0)


def forward_kernel(distances, copies, pairs_ref, count_ref, ints_ref, floats_ref, tile_ref, *refs):
    link_refs, (out_ref, seg_scratch, acc_scratch) = refs[:-3], refs[-3:]
    each = link_refs[0].shape[0] // BANDS
    owners = each * len(link_refs)
    groups = owners // 8
    index_ref, slot_ref, length_ref = ints_ref, ints_ref.at[owners:], floats_ref.at[owners:]
    place = iota((BANDS, LANES), 1) // WIDTH
    tables = []
    for group in range(groups):
        index = index_ref[group * 8 : group * 8 + 8]
        table = jnp.zeros((BANDS, LANES), jnp.float32)
        for member in range(8):
            block = group * 8 + member
            rows = slice(block % each * BANDS, (block % each + 1) * BANDS)
            picked = lane_pick(link_refs[block // each][rows], index)
            if distances:
                member = lax.axis_index("src") ^ (distances[block // each] + block % each)
            table = jnp.where(place == member, picked, table)
        tables.append(table)
    blocks = slot_ref.shape[0]
    for block in range(blocks):
        slot = jnp.broadcast_to(slot_ref[block : block + 1], (BANDS, LANES))
        value = lane_pick(tables[0], slot % LANES)
        for group in range(1, groups):
            value = jnp.where(slot // LANES == group, lane_pick(tables[group], slot % LANES), value)
        high, low = split2(value * length_ref[block : block + 1])
        seg_scratch[block] = jnp.concatenate([high, low], axis=0)
    acc_scratch[...] = jnp.zeros(acc_scratch.shape, jnp.float32)

    def multiply(seg, tile):
        rows = jnp.concatenate([only_band(seg, band) for band in range(BANDS)], axis=1)
        tiles = tile_ref[tile].reshape(BANDS * LANES, LANES)
        return jnp.dot(rows, tiles, preferred_element_type=jnp.float32)

    each_tile(
        pairs_ref,
        count_ref[0, 0],
        lambda tile: seg_scratch[pairs_ref[0, tile]],
        multiply,
        lambda tile: pairs_ref[1, tile],
        acc_scratch,
    )
    facades = acc_scratch.shape[0]
    sums = [jnp.sum(acc_scratch[block], axis=0, keepdims=True) for block in range(facades)]
    result = jnp.concatenate(sums, axis=0)
    for copy in range(copies):
        out_ref[copy * facades : (copy + 1) * facades] = result


def backward_kernel(
    hours_weight, receivers, pairs_ref, count_ref, people_ref, floats_ref, spread_ref, tile_ref, *refs
):
    part_refs, (out_ref, grad_scratch, acc_scratch) = refs[:-3], refs[-3:]
    facades = people_ref.shape[0]
    owners = out_ref.shape[0] // (receivers * ROWS)
    relay_ref, length_ref = floats_ref, floats_ref.at[owners:]
    parts = [
        ref[first : first + facades]
        for ref in part_refs
        for first in range(0, ref.shape[0], facades)
    ]
    while len(parts) > 1:
        parts = [sum(parts[k + 1 : k + 2], parts[k]) for k in range(0, len(parts), 2)]
    (total,) = parts
    total = total + 0.01 * hours_weight
    level = 60.0 + (10.0 / math.log(10.0)) * jnp.log(total / 24.0)
    people = people_ref[...].astype(jnp.float32)
    annoyed = people * (78.927 - 3.1162 * level + 0.0342 * level * level) / 100.0
    annoyed = jnp.sum(annoyed, keepdims=True)
    slope = people * (-3.1162 + 0.0684 * level) / 100.0 * (10.0 / math.log(10.0)) / total
    grads = [slope, slope * ROOT, slope * 10.0]
    pad = jnp.zeros((8, LANES), jnp.float32)
    for block in range(facades):
        rows = [jnp.broadcast_to(g[block : block + 1], (BANDS, LANES)) for g in grads]
        grad_scratch[block] = jnp.concatenate(rows + [pad], axis=0).astype(jnp.bfloat16)
    acc_scratch[...] = jnp.zeros(acc_scratch.shape, jnp.float32)

    def multiply(grad, tile):
        rows = jnp.concatenate([only_band(grad, band) for band in range(BANDS)], axis=1)
        tiles = tile_ref[tile].reshape(BANDS * LANES, LANES)
        return jnp.dot(rows, tiles, preferred_element_type=jnp.float32)

    each_tile(
        pairs_ref,
        count_ref[0, 0],
        lambda tile: grad_scratch[pairs_ref[1, tile]],
        multiply,
        lambda tile: pairs_ref[0, tile],
        acc_scratch,
    )
    used = CLASSES * BANDS
    blocks = acc_scratch.shape[0]
    high, low = [], []
    for block in range(blocks):
        value = acc_scratch[block][:used] * length_ref[block : block + 1]
        high_part = value.astype(jnp.bfloat16).astype(jnp.float32)
        high.append(high_part)
        low.append(value - high_part)
    rows = jnp.concatenate(
        [jnp.concatenate(high, axis=1), jnp.concatenate(low, axis=1)], axis=0
    ).astype(jnp.bfloat16)
    slots = jnp.dot(rows, spread_ref[...], preferred_element_type=jnp.float32)
    slots = slots[:used] + slots[used:]
    place = iota((8, LANES), 1) // WIDTH
    for group in range(owners // 8):
        lanes = slice(group * LANES, (group + 1) * LANES)
        rows = [
            swap_groups(slots[kind * BANDS : (kind + 1) * BANDS, lanes])
            for kind in range(CLASSES)
        ]
        rows.append(jnp.where(place == 0, relay_ref[group * 8 : group * 8 + 8], annoyed))
        for receiver in range(receivers):
            first = (receiver * owners + group * 8) * ROWS
            for kind in range(ROWS):
                out_ref[pl.ds(first + kind, 8, stride=ROWS), :] = rows[kind]


def finish_kernel(receivers, in_ref, table_ref, flow_out, speed_out, count_out):
    owners = in_ref.shape[0] // (receivers * ROWS)
    place, row = iota((8, LANES), 1) // WIDTH, iota((8, LANES), 0)
    used = CLASSES * BANDS
    links = jnp.zeros((2 * used, LANES), jnp.float32)
    for group in range(owners // 8):
        parts = []
        for kind in range(ROWS):
            rows = [
                in_ref[pl.ds((receiver * owners + group * 8) * ROWS + kind, 8, stride=ROWS), :]
                for receiver in range(receivers)
            ]
            total = sum(rows[1:], rows[0])
            parts.append(swap_groups(total) if kind < CLASSES else rows[0])
        if group == 0:
            count_out[...] = jnp.broadcast_to(total[0:1, LANES - 1 :], (1, LANES))
        value = jnp.concatenate(parts[:CLASSES], axis=0)
        high = value.astype(jnp.bfloat16).astype(jnp.float32)
        rows = jnp.concatenate([high, value - high], axis=0).astype(jnp.bfloat16)
        relay = lane_pick(parts[CLASSES], iota((8, LANES), 1) % WIDTH)
        relay = jnp.sum(jnp.where(place == row, relay, 0.0), axis=0, keepdims=True)
        relay = relay.astype(jnp.int32)
        spread = jnp.where(iota((LANES, LANES), 0) == relay, 1.0, 0.0).astype(jnp.bfloat16)
        links = links + lax.dot_general(rows, spread, NT, preferred_element_type=jnp.float32)
    links = links[:used] + links[used:]
    kind = hour_class(flow_out.shape)
    flow_sum = jnp.zeros(flow_out.shape, jnp.float32)
    speed_sum = jnp.zeros(flow_out.shape, jnp.float32)
    for band in range(BANDS):
        day, evening, night = [
            links[k * BANDS + band : k * BANDS + band + 1] for k in range(CLASSES)
        ]
        back = jnp.where(kind == 0, day, jnp.where(kind == 1, evening, night))
        flow_sum = flow_sum + back * table_ref[band]
        speed_sum = speed_sum + back * table_ref[BANDS + band]
    flow_out[...] = flow_sum
    speed_out[...] = speed_sum


def call(kernel, name, outs, args, scratch=()):
    space = {"smem": pltpu.SMEM, "vmem": pltpu.VMEM, "hbm": pltpu.HBM}
    return pl.pallas_call(
        kernel,
        out_shape=[
            space[place](shape, dtype) if place else jax.ShapeDtypeStruct(shape, dtype)
            for shape, dtype, place in outs
        ],
        in_specs=[pl.BlockSpec(memory_space=space[place or "smem"]) for _, place in args],
        out_specs=[pl.BlockSpec(memory_space=space[place or "vmem"]) for _, _, place in outs],
        scratch_shapes=list(scratch),
        compiler_params=pltpu.CompilerParams(vmem_limit_bytes=VMEM_BYTES),
        name=name,
    )(
        *[
            pltpu.with_memory_space_constraint(array, space[place]) if place else array
            for array, place in args
        ]
    )


def pair(array, distance):
    sources = lax.axis_size("src")
    return lax.ppermute(array, "src", [(k, k ^ distance) for k in range(sources)])


LINKS_ORDER = (4, 6, 2)
TOTALS_ORDER = (6, 4, 2)


def partners(array, distances):
    return [pair(array, distance) for distance in distances]


def shards(
    flows, speeds, seg_length, relay_list, seg_slot, tile_pairs, tile_count, attenuation, dwellings
):
    sources, receivers = lax.axis_size("src"), lax.axis_size("rcv")
    hours = flows.shape[0]
    slots = sources * WIDTH
    f32, i32, bf16 = jnp.float32, jnp.int32, jnp.bfloat16
    blocks, facades = seg_slot.shape[0] // LANES, dwellings.shape[0] // LANES
    hours_weight = sum(
        1.0 if 7 <= h < 19 else (ROOT if 19 <= h < 23 else 10.0) for h in range(hours)
    )

    def vmem(shape, dtype):
        return (shape, dtype, "vmem")

    pairwise = sources == 8
    copies = 1 if pairwise else sources
    (power,) = call(
        functools.partial(source_kernel, copies),
        "source",
        [vmem((copies * BANDS, LANES), f32)],
        [(flows, "hbm"), (speeds, "hbm")],
        [
            pltpu.VMEM((hours, LANES), f32),
            pltpu.VMEM((hours, LANES), f32),
            pltpu.SemaphoreType.DMA((2,)),
        ],
    )
    if pairwise:
        power = jnp.concatenate([power, pair(power, 1)], axis=0)
        powers = [power] + partners(power, LINKS_ORDER)
    else:
        powers = [lax.all_to_all(power, "src", 0, 0, tiled=True)]
    tables, spread, ints, floats, people, tiles, pairs = call(
        prepare_kernel,
        "prepare",
        [
            vmem((2 * BANDS, hours, LANES), f32),
            vmem((blocks * LANES, slots), bf16),
            vmem((sources + blocks, LANES), i32),
            vmem((sources + blocks, LANES), f32),
            vmem((facades, LANES), i32),
            vmem(attenuation.shape[2:], bf16),
            (tile_pairs.shape[2:], i32, "smem"),
        ],
        [
            (array, "hbm")
            for array in (
                tile_pairs[0, 0],
                flows,
                speeds,
                seg_slot.reshape(blocks, LANES),
                relay_list[0],
                seg_length.reshape(blocks, LANES),
                dwellings.reshape(facades, LANES),
                attenuation[0, 0],
            )
        ],
        [
            pltpu.VMEM((hours, LANES), f32),
            pltpu.VMEM((hours, LANES), f32),
            pltpu.VMEM((sources, WIDTH), i32),
            pltpu.VMEM((sources, LANES), i32),
            pltpu.SemaphoreType.DMA((8,)),
        ],
    )
    here = [(pairs, "smem"), (tile_count, "")]
    (part,) = call(
        functools.partial(forward_kernel, (0, *LINKS_ORDER) if pairwise else (), copies),
        "forward",
        [vmem((copies * facades, LANES), f32)],
        here + [(array, "vmem") for array in (ints, floats, tiles, *powers)],
        [
            pltpu.VMEM((blocks, 2 * BANDS, LANES), bf16),
            pltpu.VMEM((facades, 2 * BANDS, LANES), f32),
        ],
    )
    if pairwise:
        total = part + pair(part, 1)
        parts = [total] + partners(total, TOTALS_ORDER)
    else:
        parts = [lax.all_to_all(part, "src", 0, 0, tiled=True)]
    (turned,) = call(
        turn_kernel,
        "turn",
        [vmem(attenuation.shape[2:], bf16)],
        [(tile_count, ""), (tiles, "vmem"), (part, "vmem")],
    )
    (back,) = call(
        functools.partial(backward_kernel, hours_weight, receivers),
        "backward",
        [vmem((receivers * sources * ROWS, LANES), f32)],
        here + [(array, "vmem") for array in (people, floats, spread, turned, *parts)],
        [
            pltpu.VMEM((facades, 32, LANES), bf16),
            pltpu.VMEM((blocks, 32, LANES), f32),
        ],
    )
    back = back.reshape(receivers * sources, ROWS, LANES)
    back = lax.all_to_all(back, ("rcv", "src"), 0, 0, tiled=True)
    back = back.reshape(receivers * sources * ROWS, LANES)
    grad_flows, grad_speeds, annoyed = call(
        functools.partial(finish_kernel, receivers),
        "finish",
        [((hours, LANES), f32, ""), ((hours, LANES), f32, ""), ((1, LANES), f32, "")],
        [(array, "vmem") for array in (back, tables)],
    )
    return grad_flows, grad_speeds, annoyed[0, 0]


def solution(mesh):
    in_specs = (
        P(None, "src"),
        P(None, "src"),
        P("src"),
        P("src", None, None),
        P("src"),
        P("src", "rcv", None, None),
        P("src", "rcv"),
        P("src", "rcv", None, None, None, None),
        P("rcv"),
    )
    out_specs = (P(None, "src"), P(None, "src"), P())
    return jax.shard_map(shards, mesh=mesh, in_specs=in_specs, out_specs=out_specs, check_vma=False)
```

```python
import functools
import math

import jax
import jax.numpy as jnp
from jax import lax
from jax.experimental import pallas as pl
from jax.experimental.pallas import tpu as pltpu
from jax.sharding import PartitionSpec as P

rolling_base = [79.7, 85.7, 84.5, 90.2, 97.3, 93.9, 84.1, 74.3]
rolling_slope = [30.0, 41.5, 38.9, 25.7, 32.5, 37.2, 39.0, 40.0]
propel_base = [94.5, 89.2, 88.0, 85.9, 84.2, 86.9, 83.3, 76.1]
propel_slope = [-1.3, 7.2, 7.7, 8.0, 8.0, 8.0, 8.0, 8.0]
aweight_db = [-26.2, -16.1, -8.6, -3.2, 0.0, 1.2, 1.0, -1.1]

BANDS = 8
LANES = 128
CLASSES = 3
WIDTH = 16
VMEM_BYTES = 8 * 2**20
ROWS = 4
TOGETHER = 6
ROOT = math.sqrt(10.0)
DECIBEL = math.log(10.0) / 10.0
NT = (((1,), (1,)), ((), ()))


def iota(shape, axis):
    return lax.broadcasted_iota(jnp.int32, shape, axis)


def hour_class(shape):
    hour = iota(shape, 0)
    day = (hour >= 7) & (hour < 19)
    evening = (hour >= 19) & (hour < 23)
    return jnp.where(day, 0, jnp.where(evening, 1, 2))


def log10_ratio(speed_kmh):
    return jnp.log(speed_kmh / 70.0) * (1.0 / math.log(10.0))


def band_terms(speed_kmh, log_ratio):
    terms, propels = [], {}
    for band in range(BANDS):
        shift = aweight_db[band] - 90.0
        rolling = jnp.exp(
            DECIBEL * (rolling_base[band] + shift) + (DECIBEL * rolling_slope[band]) * log_ratio
        )
        slope = propel_slope[band]
        if slope not in propels:
            propels[slope] = jnp.exp((DECIBEL * slope / 70.0) * (speed_kmh - 70.0))
        terms.append((rolling, math.exp(DECIBEL * (propel_base[band] + shift)) * propels[slope]))
    return terms


def lane_pick(table, index):
    return jnp.take_along_axis(table, index, axis=1, mode="promise_in_bounds")


def swap_groups(block):
    row, lane = iota((8, LANES), 0), iota((8, LANES), 1)
    block = lane_pick(block, (lane + LANES - WIDTH * row) % LANES)
    block = jnp.take_along_axis(
        block, (lane // WIDTH + 8 - row) % 8, axis=0, mode="promise_in_bounds"
    )
    return lane_pick(block, (lane + WIDTH * row) % LANES)


def each_tile(pairs_ref, count, read, multiply, write, acc_ref):
    def step(turn, carry):
        added = []
        for place in range(TOGETHER):
            number = turn * TOGETHER + place
            tile = jnp.minimum(number, count - 1)
            value = read(tile)
            value = jnp.where(number < count, value, jnp.zeros_like(value))
            added.append((write(tile), multiply(value, tile)))
        for block, value in added:
            acc_ref[block] += value
        return carry

    lax.fori_loop(0, (count + TOGETHER - 1) // TOGETHER, step, 0)


def stack_sums(blocks):
    row = iota((8, LANES), 0)
    for distance in (4, 2, 1):
        half = len(blocks) // 2
        near = (row & distance) == 0
        blocks = [
            jnp.where(near, first, second)
            + jnp.take_along_axis(
                jnp.where(near, second, first), row ^ distance, axis=0, mode="promise_in_bounds"
            )
            for first, second in zip(blocks[:half], blocks[half:])
        ]
    return blocks[0]


def only_band(value, band):
    row = iota(value.shape, 0) % BANDS
    return jnp.where(row == band, value, jnp.zeros_like(value))


def split2(value):
    high = value.astype(jnp.bfloat16)
    low = (value - high.astype(jnp.float32)).astype(jnp.bfloat16)
    return high, low


def source_kernel(copies, flow_hbm, speed_hbm, out_ref, flow_ref, speed_ref, sems):
    fetches = [
        pltpu.make_async_copy(speed_hbm, speed_ref, sems.at[0]),
        pltpu.make_async_copy(flow_hbm, flow_ref, sems.at[1]),
    ]
    for fetch in fetches:
        fetch.start()
    fetches[0].wait()
    speed = speed_ref[...]
    speed_kmh = 100.0 * speed
    log_ratio = log10_ratio(speed_kmh)
    terms = band_terms(speed_kmh, log_ratio)
    kind = hour_class(speed.shape)
    weight = jnp.where(kind == 0, 1.0, jnp.where(kind == 1, ROOT, 10.0)) / speed_kmh
    fetches[1].wait()
    scale = weight * flow_ref[...]
    sums = []
    for rolling, propel in terms:
        power = scale * (rolling + propel)
        sums.append(sum(power[k : k + 8] for k in range(8, power.shape[0], 8)) + power[:8])
    result = stack_sums(sums)
    for copy in range(copies):
        out_ref[copy * BANDS : (copy + 1) * BANDS] = result


def prepare_kernel(
    pairs_hbm, flow_hbm, speed_hbm, slot_hbm, relay_hbm, length_hbm, people_hbm, tile_hbm,
    table_ref, spread_ref, ints_ref, floats_ref, people_ref, tile_ref, pairs_ref, flow_ref, speed_ref, relay_ref, relay_scratch, sems,
):
    owners, blocks = relay_hbm.shape[0], slot_hbm.shape[0]
    index_ref, slot_ref = ints_ref.at[:owners], ints_ref.at[owners:]
    wide_ref, length_ref = floats_ref.at[:owners], floats_ref.at[owners:]
    moves = [
        (flow_hbm, flow_ref),
        (speed_hbm, speed_ref),
        (relay_hbm, relay_ref),
        (slot_hbm, slot_ref),
        (pairs_hbm, pairs_ref),
        (length_hbm, length_ref),
        (people_hbm, people_ref),
        (tile_hbm, tile_ref),
    ]
    fetches = [
        pltpu.make_async_copy(start, end, sems.at[k]) for k, (start, end) in enumerate(moves)
    ]
    for fetch in fetches:
        fetch.start()
    for fetch in fetches[:4]:
        fetch.wait()
    relay_scratch[...] = jnp.zeros(relay_scratch.shape, jnp.int32)
    relay_scratch[:, :WIDTH] = relay_ref[...]
    lane, row = iota((8, LANES), 1), iota((8, LANES), 0)
    for group in range(owners // 8):
        rows = slice(group * 8, group * 8 + 8)
        wide = lane_pick(relay_scratch[rows], lane % WIDTH)
        wide_ref[rows] = wide.astype(jnp.float32)
        picked = jnp.where(lane // WIDTH == row, jnp.maximum(wide, 0), 0)
        picked = jnp.sum(picked, axis=0, keepdims=True)
        index_ref[rows] = jnp.broadcast_to(picked, (8, LANES))
    flow, speed = flow_ref[...], speed_ref[...]
    speed_kmh = 100.0 * speed
    terms = band_terms(speed_kmh, log10_ratio(speed_kmh))
    per_flow = 1.0 / speed_kmh
    factor = flow * per_flow
    inverse = 1.0 / speed
    for band, (rolling, propel) in enumerate(terms):
        table_ref[band] = per_flow * (rolling + propel)
        table_ref[BANDS + band] = factor * (
            rolling * (rolling_slope[band] / 10.0 - 1.0) * inverse
            + propel * (math.log(10.0) * propel_slope[band] / 7.0 - inverse)
        )
    slots = spread_ref.shape[1]
    for block in range(blocks):
        same = iota((slots, LANES), 0) == slot_ref[block : block + 1]
        spread_ref[block * LANES : (block + 1) * LANES] = (
            jnp.where(same, 1.0, 0.0).T.astype(jnp.bfloat16)
        )
    for fetch in fetches[4:]:
        fetch.wait()


def turn_kernel(count_ref, tile_ref, part_ref, out_ref):
    def step(tile, carry):
        for band in range(BANDS):
            out_ref[tile, band] = tile_ref[tile, band].T
        return carry

    lax.fori_loop(0, count_ref[0, 0], step, 0)


def forward_kernel(shared, copies, pairs_ref, count_ref, ints_ref, floats_ref, tile_ref, *refs):
    link_refs, (out_ref, seg_scratch, acc_scratch) = refs[:-3], refs[-3:]
    each = link_refs[0].shape[0] // BANDS
    owners = each * len(link_refs)
    groups = owners // 8
    index_ref, slot_ref, length_ref = ints_ref, ints_ref.at[owners:], floats_ref.at[owners:]
    place = iota((BANDS, LANES), 1) // WIDTH
    tables = []
    for group in range(groups):
        index = index_ref[group * 8 : group * 8 + 8]
        table = jnp.zeros((BANDS, LANES), jnp.float32)
        for member in range(8):
            block = group * 8 + member
            rows = slice(block % each * BANDS, (block % each + 1) * BANDS)
            picked = lane_pick(link_refs[block // each][rows], index)
            if shared:
                member = share_owner(block // each, block % each)
            table = jnp.where(place == member, picked, table)
        tables.append(table)
    blocks = slot_ref.shape[0]
    for block in range(blocks):
        slot = jnp.broadcast_to(slot_ref[block : block + 1], (BANDS, LANES))
        value = lane_pick(tables[0], slot % LANES)
        for group in range(1, groups):
            value = jnp.where(slot // LANES == group, lane_pick(tables[group], slot % LANES), value)
        high, low = split2(value * length_ref[block : block + 1])
        seg_scratch[block] = jnp.concatenate([high, low], axis=0)
    acc_scratch[...] = jnp.zeros(acc_scratch.shape, jnp.float32)

    def multiply(seg, tile):
        rows = jnp.concatenate([only_band(seg, band) for band in range(BANDS)], axis=1)
        tiles = tile_ref[tile].reshape(BANDS * LANES, LANES)
        return jnp.dot(rows, tiles, preferred_element_type=jnp.float32)

    each_tile(
        pairs_ref,
        count_ref[0, 0],
        lambda tile: seg_scratch[pairs_ref[0, tile]],
        multiply,
        lambda tile: pairs_ref[1, tile],
        acc_scratch,
    )
    facades = acc_scratch.shape[0]
    result = stack_sums([acc_scratch[block, :8] + acc_scratch[block, 8:] for block in range(facades)])
    for copy in range(copies):
        out_ref[copy * facades : (copy + 1) * facades] = result


def backward_kernel(
    hours, hours_weight, receivers, pairs_ref, count_ref, people_ref, floats_ref, spread_ref, tile_ref, *refs
):
    part_refs, (out_ref, grad_scratch, acc_scratch) = refs[:-3], refs[-3:]
    facades = people_ref.shape[0]
    owners = out_ref.shape[0] // (receivers * ROWS)
    relay_ref, length_ref = floats_ref, floats_ref.at[owners:]
    parts = [
        ref[first : first + facades]
        for ref in part_refs
        for first in range(0, ref.shape[0], facades)
    ]
    while len(parts) > 1:
        parts = [sum(parts[k + 1 : k + 2], parts[k]) for k in range(0, len(parts), 2)]
    (total,) = parts
    total = total + 0.01 * hours_weight
    level = (60.0 - 10.0 * math.log10(hours)) + (10.0 / math.log(10.0)) * jnp.log(total)
    people = people_ref[...].astype(jnp.float32)
    rise = (0.1 / math.log(10.0)) * people * (-3.1162 + 0.0684 * level)
    slope = rise / total
    grads = [slope, slope * ROOT, slope * 10.0]
    pad = jnp.zeros((8, LANES), jnp.float32)
    for block in range(facades):
        rows = [jnp.broadcast_to(g[block : block + 1], (BANDS, LANES)) for g in grads]
        grad_scratch[block] = jnp.concatenate(rows + [pad], axis=0).astype(jnp.bfloat16)
    acc_scratch[...] = jnp.zeros(acc_scratch.shape, jnp.float32)

    def multiply(grad, tile):
        rows = jnp.concatenate([only_band(grad, band) for band in range(BANDS)], axis=1)
        tiles = tile_ref[tile].reshape(BANDS * LANES, LANES)
        return jnp.dot(rows, tiles, preferred_element_type=jnp.float32)

    each_tile(
        pairs_ref,
        count_ref[0, 0],
        lambda tile: grad_scratch[pairs_ref[1, tile]],
        multiply,
        lambda tile: pairs_ref[0, tile],
        acc_scratch,
    )
    annoyed = (0.01 * people) * (78.927 - 3.1162 * level + 0.0342 * level * level)
    annoyed = jnp.sum(annoyed, keepdims=True)
    used = CLASSES * BANDS
    blocks = acc_scratch.shape[0]
    high, low = [], []
    for block in range(blocks):
        value = acc_scratch[block][:used] * length_ref[block : block + 1]
        high_part = value.astype(jnp.bfloat16).astype(jnp.float32)
        high.append(high_part)
        low.append(value - high_part)
    rows = jnp.concatenate(
        [jnp.concatenate(high, axis=1), jnp.concatenate(low, axis=1)], axis=0
    ).astype(jnp.bfloat16)
    slots = jnp.dot(rows, spread_ref[...], preferred_element_type=jnp.float32)
    slots = slots[:used] + slots[used:]
    place = iota((8, LANES), 1) // WIDTH
    for group in range(owners // 8):
        lanes = slice(group * LANES, (group + 1) * LANES)
        rows = [
            swap_groups(slots[kind * BANDS : (kind + 1) * BANDS, lanes])
            for kind in range(CLASSES)
        ]
        rows.append(jnp.where(place == 0, relay_ref[group * 8 : group * 8 + 8], annoyed))
        for receiver in range(receivers):
            first = (receiver * owners + group * 8) * ROWS
            for kind in range(ROWS):
                out_ref[pl.ds(first + kind, 8, stride=ROWS), :] = rows[kind]


def finish_kernel(receivers, in_ref, table_ref, flow_out, speed_out, count_out):
    owners = in_ref.shape[0] // (receivers * ROWS)
    place, row = iota((8, LANES), 1) // WIDTH, iota((8, LANES), 0)
    used = CLASSES * BANDS
    links = jnp.zeros((2 * used, LANES), jnp.float32)
    for group in range(owners // 8):
        parts = []
        for kind in range(ROWS):
            rows = [
                in_ref[pl.ds((receiver * owners + group * 8) * ROWS + kind, 8, stride=ROWS), :]
                for receiver in range(receivers)
            ]
            total = sum(rows[1:], rows[0])
            parts.append(swap_groups(total) if kind < CLASSES else rows[0])
        if group == 0:
            count_out[...] = jnp.broadcast_to(total[0:1, LANES - 1 :], (1, LANES))
        value = jnp.concatenate(parts[:CLASSES], axis=0)
        high = value.astype(jnp.bfloat16).astype(jnp.float32)
        rows = jnp.concatenate([high, value - high], axis=0).astype(jnp.bfloat16)
        relay = lane_pick(parts[CLASSES], iota((8, LANES), 1) % WIDTH)
        relay = jnp.sum(jnp.where(place == row, relay, 0.0), axis=0, keepdims=True)
        relay = relay.astype(jnp.int32)
        spread = jnp.where(iota((LANES, LANES), 0) == relay, 1.0, 0.0).astype(jnp.bfloat16)
        links = links + lax.dot_general(rows, spread, NT, preferred_element_type=jnp.float32)
    links = links[:used] + links[used:]
    kind = hour_class(flow_out.shape)
    flow_sum = jnp.zeros(flow_out.shape, jnp.float32)
    speed_sum = jnp.zeros(flow_out.shape, jnp.float32)
    for band in range(BANDS):
        day, evening, night = [
            links[k * BANDS + band : k * BANDS + band + 1] for k in range(CLASSES)
        ]
        back = jnp.where(kind == 0, day, jnp.where(kind == 1, evening, night))
        flow_sum = flow_sum + back * table_ref[band]
        speed_sum = speed_sum + back * table_ref[BANDS + band]
    flow_out[...] = flow_sum
    speed_out[...] = speed_sum


def call(kernel, name, outs, args, scratch=()):
    space = {"smem": pltpu.SMEM, "vmem": pltpu.VMEM, "hbm": pltpu.HBM}
    return pl.pallas_call(
        kernel,
        out_shape=[
            space[place](shape, dtype) if place else jax.ShapeDtypeStruct(shape, dtype)
            for shape, dtype, place in outs
        ],
        in_specs=[pl.BlockSpec(memory_space=space[place or "smem"]) for _, place in args],
        out_specs=[pl.BlockSpec(memory_space=space[place or "vmem"]) for _, _, place in outs],
        scratch_shapes=list(scratch),
        compiler_params=pltpu.CompilerParams(vmem_limit_bytes=VMEM_BYTES),
        name=name,
    )(
        *[
            pltpu.with_memory_space_constraint(array, space[place]) if place else array
            for array, place in args
        ]
    )


def pair(array, *distances):
    sources = lax.axis_size("src")
    return lax.ppermute(
        array, "src", [(k, k ^ distances[k % len(distances)]) for k in range(sources)]
    )


FAR = (4, 6)


def exchange(array, work):
    far, near = pair(array, *FAR), pair(array, 2)
    if work:
        near, far, *work = lax.optimization_barrier((near, far, *work))
    return [far, pair(far, 1), near, array], work


def share_owner(share, member):
    own = lax.axis_index("src")
    odd = own % 2
    first, second = FAR[0] + (FAR[1] - FAR[0]) * odd, FAR[1] + (FAR[0] - FAR[1]) * odd
    return own ^ (first, second ^ 1, 2, 0)[share] ^ member


def shards(
    flows, speeds, seg_length, relay_list, seg_slot, tile_pairs, tile_count, attenuation, dwellings
):
    sources, receivers = lax.axis_size("src"), lax.axis_size("rcv")
    hours = flows.shape[0]
    slots = sources * WIDTH
    f32, i32, bf16 = jnp.float32, jnp.int32, jnp.bfloat16
    blocks, facades = seg_slot.shape[0] // LANES, dwellings.shape[0] // LANES
    hours_weight = sum(
        1.0 if 7 <= h < 19 else (ROOT if 19 <= h < 23 else 10.0) for h in range(hours)
    )

    def vmem(shape, dtype):
        return (shape, dtype, "vmem")

    pairwise = sources == 8
    copies = 1 if pairwise else sources
    (power,) = call(
        functools.partial(source_kernel, copies),
        "source",
        [vmem((copies * BANDS, LANES), f32)],
        [(flows, "hbm"), (speeds, "hbm")],
        [
            pltpu.VMEM((hours, LANES), f32),
            pltpu.VMEM((hours, LANES), f32),
            pltpu.SemaphoreType.DMA((2,)),
        ],
    )
    tables, spread, ints, floats, people, tiles, pairs = call(
        prepare_kernel,
        "prepare",
        [
            vmem((2 * BANDS, hours, LANES), f32),
            vmem((blocks * LANES, slots), bf16),
            vmem((sources + blocks, LANES), i32),
            vmem((sources + blocks, LANES), f32),
            vmem((facades, LANES), i32),
            vmem(attenuation.shape[2:], bf16),
            (tile_pairs.shape[2:], i32, "smem"),
        ],
        [
            (array, "hbm")
            for array in (
                tile_pairs[0, 0],
                flows,
                speeds,
                seg_slot.reshape(blocks, LANES),
                relay_list[0],
                seg_length.reshape(blocks, LANES),
                dwellings.reshape(facades, LANES),
                attenuation[0, 0],
            )
        ],
        [
            pltpu.VMEM((hours, LANES), f32),
            pltpu.VMEM((hours, LANES), f32),
            pltpu.VMEM((sources, WIDTH), i32),
            pltpu.VMEM((sources, LANES), i32),
            pltpu.SemaphoreType.DMA((8,)),
        ],
    )
    if pairwise:
        power = jnp.concatenate([power, pair(power, 1)], axis=0)
        powers, (ints,) = exchange(power, [ints])
    else:
        powers = [lax.all_to_all(power, "src", 0, 0, tiled=True)]
    here = [(pairs, "smem"), (tile_count, "")]
    (part,) = call(
        functools.partial(forward_kernel, pairwise, copies),
        "forward",
        [vmem((copies * facades, LANES), f32)],
        here + [(array, "vmem") for array in (ints, floats, tiles, *powers)],
        [
            pltpu.VMEM((blocks, 2 * BANDS, LANES), bf16),
            pltpu.VMEM((facades, 2 * BANDS, LANES), f32),
        ],
    )
    (turned,) = call(
        turn_kernel,
        "turn",
        [vmem(attenuation.shape[2:], bf16)],
        [(tile_count, ""), (tiles, "vmem"), (part, "vmem")],
    )
    if pairwise:
        total = part + pair(part, 1)
        parts, _ = exchange(total, [])
    else:
        parts = [lax.all_to_all(part, "src", 0, 0, tiled=True)]
    (back,) = call(
        functools.partial(backward_kernel, hours, hours_weight, receivers),
        "backward",
        [vmem((receivers * sources * ROWS, LANES), f32)],
        here + [(array, "vmem") for array in (people, floats, spread, turned, *parts)],
        [
            pltpu.VMEM((facades, 32, LANES), bf16),
            pltpu.VMEM((blocks, 32, LANES), f32),
        ],
    )
    back = back.reshape(receivers * sources, ROWS, LANES)
    back = lax.all_to_all(back, ("rcv", "src"), 0, 0, tiled=True)
    back = back.reshape(receivers * sources * ROWS, LANES)
    grad_flows, grad_speeds, annoyed = call(
        functools.partial(finish_kernel, receivers),
        "finish",
        [((hours, LANES), f32, ""), ((hours, LANES), f32, ""), ((1, LANES), f32, "")],
        [(array, "vmem") for array in (back, tables)],
    )
    return grad_flows, grad_speeds, annoyed[0, 0]


def solution(mesh):
    in_specs = (
        P(None, "src"),
        P(None, "src"),
        P("src"),
        P("src", None, None),
        P("src"),
        P("src", "rcv", None, None),
        P("src", "rcv"),
        P("src", "rcv", None, None, None, None),
        P("rcv"),
    )
    out_specs = (P(None, "src"), P(None, "src"), P())
    return jax.shard_map(shards, mesh=mesh, in_specs=in_specs, out_specs=out_specs, check_vma=False)
```

```python
import functools
import math

import jax
import jax.numpy as jnp
from jax import lax
from jax.experimental import pallas as pl
from jax.experimental.pallas import tpu as pltpu
from jax.sharding import PartitionSpec as P

rolling_base = [79.7, 85.7, 84.5, 90.2, 97.3, 93.9, 84.1, 74.3]
rolling_slope = [30.0, 41.5, 38.9, 25.7, 32.5, 37.2, 39.0, 40.0]
propel_base = [94.5, 89.2, 88.0, 85.9, 84.2, 86.9, 83.3, 76.1]
propel_slope = [-1.3, 7.2, 7.7, 8.0, 8.0, 8.0, 8.0, 8.0]
aweight_db = [-26.2, -16.1, -8.6, -3.2, 0.0, 1.2, 1.0, -1.1]

BANDS = 8
LANES = 128
CLASSES = 3
WIDTH = 16
VMEM_BYTES = 8 * 2**20
ROWS = 4
TOGETHER = 6
ROOT = math.sqrt(10.0)
DECIBEL = math.log(10.0) / 10.0
NT = (((1,), (1,)), ((), ()))


def iota(shape, axis):
    return lax.broadcasted_iota(jnp.int32, shape, axis)


def hour_class(shape):
    hour = iota(shape, 0)
    day = (hour >= 7) & (hour < 19)
    evening = (hour >= 19) & (hour < 23)
    return jnp.where(day, 0, jnp.where(evening, 1, 2))


def log10_ratio(speed_kmh):
    return jnp.log(speed_kmh / 70.0) * (1.0 / math.log(10.0))


def band_terms(speed_kmh, log_ratio):
    terms, propels = [], {}
    for band in range(BANDS):
        shift = aweight_db[band] - 90.0
        rolling = jnp.exp(
            DECIBEL * (rolling_base[band] + shift) + (DECIBEL * rolling_slope[band]) * log_ratio
        )
        slope = propel_slope[band]
        if slope not in propels:
            propels[slope] = jnp.exp((DECIBEL * slope / 70.0) * (speed_kmh - 70.0))
        terms.append((rolling, math.exp(DECIBEL * (propel_base[band] + shift)) * propels[slope]))
    return terms


def lane_pick(table, index):
    return jnp.take_along_axis(table, index, axis=1, mode="promise_in_bounds")


def swap_groups(block):
    row, lane = iota((8, LANES), 0), iota((8, LANES), 1)
    block = lane_pick(block, (lane + LANES - WIDTH * row) % LANES)
    block = jnp.take_along_axis(
        block, (lane // WIDTH + 8 - row) % 8, axis=0, mode="promise_in_bounds"
    )
    return lane_pick(block, (lane + WIDTH * row) % LANES)


def each_tile(pairs_ref, count, read, multiply, write, acc_ref):
    def step(turn, carry):
        added = []
        for place in range(TOGETHER):
            number = turn * TOGETHER + place
            tile = jnp.minimum(number, count - 1)
            value = read(tile)
            value = jnp.where(number < count, value, jnp.zeros_like(value))
            added.append((write(tile), multiply(value, tile)))
        for block, value in added:
            acc_ref[block] += value
        return carry

    lax.fori_loop(0, (count + TOGETHER - 1) // TOGETHER, step, 0)


def stack_sums(blocks):
    row = iota((8, LANES), 0)
    for distance in (4, 2, 1):
        half = len(blocks) // 2
        near = (row & distance) == 0
        blocks = [
            jnp.where(near, first, second)
            + jnp.take_along_axis(
                jnp.where(near, second, first), row ^ distance, axis=0, mode="promise_in_bounds"
            )
            for first, second in zip(blocks[:half], blocks[half:])
        ]
    return blocks[0]


def only_band(value, band):
    row = iota(value.shape, 0) % BANDS
    return jnp.where(row == band, value, jnp.zeros_like(value))


def split2(value):
    high = value.astype(jnp.bfloat16)
    low = (value - high.astype(jnp.float32)).astype(jnp.bfloat16)
    return high, low


def source_kernel(copies, flow_hbm, speed_hbm, out_ref, flow_ref, speed_ref, sems):
    fetches = [
        pltpu.make_async_copy(speed_hbm, speed_ref, sems.at[0]),
        pltpu.make_async_copy(flow_hbm, flow_ref, sems.at[1]),
    ]
    for fetch in fetches:
        fetch.start()
    fetches[0].wait()
    speed = speed_ref[...]
    speed_kmh = 100.0 * speed
    log_ratio = log10_ratio(speed_kmh)
    terms = band_terms(speed_kmh, log_ratio)
    kind = hour_class(speed.shape)
    weight = jnp.where(kind == 0, 1.0, jnp.where(kind == 1, ROOT, 10.0)) / speed_kmh
    fetches[1].wait()
    scale = weight * flow_ref[...]
    sums = []
    for rolling, propel in terms:
        power = scale * (rolling + propel)
        sums.append(sum(power[k : k + 8] for k in range(8, power.shape[0], 8)) + power[:8])
    result = stack_sums(sums)
    for copy in range(copies):
        out_ref[copy * BANDS : (copy + 1) * BANDS] = result


def prepare_kernel(
    pairs_hbm, flow_hbm, speed_hbm, slot_hbm, relay_hbm, length_hbm, people_hbm, tile_hbm,
    table_ref, spread_ref, ints_ref, floats_ref, people_ref, tile_ref, pairs_ref, flow_ref, speed_ref, relay_ref, relay_scratch, sems,
):
    owners, blocks = relay_hbm.shape[0], slot_hbm.shape[0]
    index_ref, slot_ref = ints_ref.at[:owners], ints_ref.at[owners:]
    wide_ref, length_ref = floats_ref.at[:owners], floats_ref.at[owners:]
    moves = [
        (flow_hbm, flow_ref),
        (speed_hbm, speed_ref),
        (relay_hbm, relay_ref),
        (slot_hbm, slot_ref),
        (pairs_hbm, pairs_ref),
        (length_hbm, length_ref),
        (people_hbm, people_ref),
        (tile_hbm, tile_ref),
    ]
    fetches = [
        pltpu.make_async_copy(start, end, sems.at[k]) for k, (start, end) in enumerate(moves)
    ]
    for fetch in fetches:
        fetch.start()
    for fetch in fetches[:4]:
        fetch.wait()
    relay_scratch[...] = jnp.zeros(relay_scratch.shape, jnp.int32)
    relay_scratch[:, :WIDTH] = relay_ref[...]
    lane, row = iota((8, LANES), 1), iota((8, LANES), 0)
    for group in range(owners // 8):
        rows = slice(group * 8, group * 8 + 8)
        wide = lane_pick(relay_scratch[rows], lane % WIDTH)
        wide_ref[rows] = wide.astype(jnp.float32)
        picked = jnp.where(lane // WIDTH == row, jnp.maximum(wide, 0), 0)
        picked = jnp.sum(picked, axis=0, keepdims=True)
        index_ref[rows] = jnp.broadcast_to(picked, (8, LANES))
    flow, speed = flow_ref[...], speed_ref[...]
    speed_kmh = 100.0 * speed
    terms = band_terms(speed_kmh, log10_ratio(speed_kmh))
    per_flow = 1.0 / speed_kmh
    factor = flow * per_flow
    inverse = 1.0 / speed
    for band, (rolling, propel) in enumerate(terms):
        table_ref[band] = per_flow * (rolling + propel)
        table_ref[BANDS + band] = factor * (
            rolling * (rolling_slope[band] / 10.0 - 1.0) * inverse
            + propel * (math.log(10.0) * propel_slope[band] / 7.0 - inverse)
        )
    slots = spread_ref.shape[1]
    for block in range(blocks):
        same = iota((slots, LANES), 0) == slot_ref[block : block + 1]
        spread_ref[block * LANES : (block + 1) * LANES] = (
            jnp.where(same, 1.0, 0.0).T.astype(jnp.bfloat16)
        )
    for fetch in fetches[4:]:
        fetch.wait()


def turn_kernel(count_ref, tile_ref, part_ref, out_ref):
    def step(tile, carry):
        for band in range(BANDS):
            out_ref[tile, band] = tile_ref[tile, band].T
        return carry

    lax.fori_loop(0, count_ref[0, 0], step, 0)


def forward_kernel(shared, copies, pairs_ref, count_ref, ints_ref, floats_ref, tile_ref, *refs):
    link_refs, (out_ref, seg_scratch, acc_scratch) = refs[:-3], refs[-3:]
    each = link_refs[0].shape[0] // BANDS
    owners = each * len(link_refs)
    groups = owners // 8
    index_ref, slot_ref, length_ref = ints_ref, ints_ref.at[owners:], floats_ref.at[owners:]
    place = iota((BANDS, LANES), 1) // WIDTH
    tables = []
    for group in range(groups):
        index = index_ref[group * 8 : group * 8 + 8]
        table = jnp.zeros((BANDS, LANES), jnp.float32)
        for member in range(8):
            block = group * 8 + member
            rows = slice(block % each * BANDS, (block % each + 1) * BANDS)
            picked = lane_pick(link_refs[block // each][rows], index)
            if shared:
                member = share_owner(block // each, block % each)
            table = jnp.where(place == member, picked, table)
        tables.append(table)
    blocks = slot_ref.shape[0]
    for block in range(blocks):
        slot = jnp.broadcast_to(slot_ref[block : block + 1], (BANDS, LANES))
        value = lane_pick(tables[0], slot % LANES)
        for group in range(1, groups):
            value = jnp.where(slot // LANES == group, lane_pick(tables[group], slot % LANES), value)
        high, low = split2(value * length_ref[block : block + 1])
        seg_scratch[block] = jnp.concatenate([high, low], axis=0)
    acc_scratch[...] = jnp.zeros(acc_scratch.shape, jnp.float32)

    def multiply(seg, tile):
        rows = jnp.concatenate([only_band(seg, band) for band in range(BANDS)], axis=1)
        tiles = tile_ref[tile].reshape(BANDS * LANES, LANES)
        return jnp.dot(rows, tiles, preferred_element_type=jnp.float32)

    each_tile(
        pairs_ref,
        count_ref[0, 0],
        lambda tile: seg_scratch[pairs_ref[0, tile]],
        multiply,
        lambda tile: pairs_ref[1, tile],
        acc_scratch,
    )
    facades = acc_scratch.shape[0]
    result = stack_sums([acc_scratch[block, :8] + acc_scratch[block, 8:] for block in range(facades)])
    for copy in range(copies):
        out_ref[copy * facades : (copy + 1) * facades] = result


def backward_kernel(
    hours, hours_weight, receivers, pairs_ref, count_ref, people_ref, floats_ref, spread_ref, tile_ref, *refs
):
    part_refs, (out_ref, grad_scratch, acc_scratch) = refs[:-3], refs[-3:]
    facades = people_ref.shape[0]
    owners = out_ref.shape[0] // (receivers * ROWS)
    relay_ref, length_ref = floats_ref, floats_ref.at[owners:]
    parts = [
        ref[first : first + facades]
        for ref in part_refs
        for first in range(0, ref.shape[0], facades)
    ]
    while len(parts) > 1:
        parts = [sum(parts[k + 1 : k + 2], parts[k]) for k in range(0, len(parts), 2)]
    (total,) = parts
    total = total + 0.01 * hours_weight
    level = (60.0 - 10.0 * math.log10(hours)) + (10.0 / math.log(10.0)) * jnp.log(total)
    people = people_ref[...].astype(jnp.float32)
    rise = (0.1 / math.log(10.0)) * people * (-3.1162 + 0.0684 * level)
    slope = rise / total
    grads = [slope, slope * ROOT, slope * 10.0]
    pad = jnp.zeros((8, LANES), jnp.float32)
    for block in range(facades):
        rows = [jnp.broadcast_to(g[block : block + 1], (BANDS, LANES)) for g in grads]
        grad_scratch[block] = jnp.concatenate(rows + [pad], axis=0).astype(jnp.bfloat16)
    acc_scratch[...] = jnp.zeros(acc_scratch.shape, jnp.float32)

    def multiply(grad, tile):
        rows = jnp.concatenate([only_band(grad, band) for band in range(BANDS)], axis=1)
        tiles = tile_ref[tile].reshape(BANDS * LANES, LANES)
        return jnp.dot(rows, tiles, preferred_element_type=jnp.float32)

    each_tile(
        pairs_ref,
        count_ref[0, 0],
        lambda tile: grad_scratch[pairs_ref[1, tile]],
        multiply,
        lambda tile: pairs_ref[0, tile],
        acc_scratch,
    )
    annoyed = (0.01 * people) * (78.927 - 3.1162 * level + 0.0342 * level * level)
    annoyed = jnp.sum(annoyed, keepdims=True)
    used = CLASSES * BANDS
    blocks = acc_scratch.shape[0]
    high, low = [], []
    for block in range(blocks):
        value = acc_scratch[block][:used] * length_ref[block : block + 1]
        high_part = value.astype(jnp.bfloat16).astype(jnp.float32)
        high.append(high_part)
        low.append(value - high_part)
    rows = jnp.concatenate(
        [jnp.concatenate(high, axis=1), jnp.concatenate(low, axis=1)], axis=0
    ).astype(jnp.bfloat16)
    slots = jnp.dot(rows, spread_ref[...], preferred_element_type=jnp.float32)
    slots = slots[:used] + slots[used:]
    place = iota((8, LANES), 1) // WIDTH
    for group in range(owners // 8):
        lanes = slice(group * LANES, (group + 1) * LANES)
        rows = [
            swap_groups(slots[kind * BANDS : (kind + 1) * BANDS, lanes])
            for kind in range(CLASSES)
        ]
        rows.append(jnp.where(place == 0, relay_ref[group * 8 : group * 8 + 8], annoyed))
        for receiver in range(receivers):
            first = (receiver * owners + group * 8) * ROWS
            for kind in range(ROWS):
                out_ref[pl.ds(first + kind, 8, stride=ROWS), :] = rows[kind]


def finish_kernel(receivers, in_ref, table_ref, flow_out, speed_out, count_out):
    owners = in_ref.shape[0] // (receivers * ROWS)
    place, row = iota((8, LANES), 1) // WIDTH, iota((8, LANES), 0)
    used = CLASSES * BANDS
    links = jnp.zeros((2 * used, LANES), jnp.float32)
    for group in range(owners // 8):
        parts = []
        for kind in range(ROWS):
            rows = [
                in_ref[pl.ds((receiver * owners + group * 8) * ROWS + kind, 8, stride=ROWS), :]
                for receiver in range(receivers)
            ]
            total = sum(rows[1:], rows[0])
            parts.append(swap_groups(total) if kind < CLASSES else rows[0])
        if group == 0:
            count_out[...] = jnp.broadcast_to(total[0:1, LANES - 1 :], (1, LANES))
        value = jnp.concatenate(parts[:CLASSES], axis=0)
        high = value.astype(jnp.bfloat16).astype(jnp.float32)
        rows = jnp.concatenate([high, value - high], axis=0).astype(jnp.bfloat16)
        relay = lane_pick(parts[CLASSES], iota((8, LANES), 1) % WIDTH)
        relay = jnp.sum(jnp.where(place == row, relay, 0.0), axis=0, keepdims=True)
        relay = relay.astype(jnp.int32)
        spread = jnp.where(iota((LANES, LANES), 0) == relay, 1.0, 0.0).astype(jnp.bfloat16)
        links = links + lax.dot_general(rows, spread, NT, preferred_element_type=jnp.float32)
    links = links[:used] + links[used:]
    kind = hour_class(flow_out.shape)
    flow_sum = jnp.zeros(flow_out.shape, jnp.float32)
    speed_sum = jnp.zeros(flow_out.shape, jnp.float32)
    for band in range(BANDS):
        day, evening, night = [
            links[k * BANDS + band : k * BANDS + band + 1] for k in range(CLASSES)
        ]
        back = jnp.where(kind == 0, day, jnp.where(kind == 1, evening, night))
        flow_sum = flow_sum + back * table_ref[band]
        speed_sum = speed_sum + back * table_ref[BANDS + band]
    flow_out[...] = flow_sum
    speed_out[...] = speed_sum


def call(kernel, name, outs, args, scratch=()):
    space = {"smem": pltpu.SMEM, "vmem": pltpu.VMEM, "hbm": pltpu.HBM}
    return pl.pallas_call(
        kernel,
        out_shape=[
            space[place](shape, dtype) if place else jax.ShapeDtypeStruct(shape, dtype)
            for shape, dtype, place in outs
        ],
        in_specs=[pl.BlockSpec(memory_space=space[place or "smem"]) for _, place in args],
        out_specs=[pl.BlockSpec(memory_space=space[place or "vmem"]) for _, _, place in outs],
        scratch_shapes=list(scratch),
        compiler_params=pltpu.CompilerParams(vmem_limit_bytes=VMEM_BYTES),
        name=name,
    )(
        *[
            pltpu.with_memory_space_constraint(array, space[place]) if place else array
            for array, place in args
        ]
    )


def pair(array, *distances):
    sources = lax.axis_size("src")
    return lax.ppermute(
        array, "src", [(k, k ^ distances[k % len(distances)]) for k in range(sources)]
    )


FAR = (4, 6)


def exchange(array, work):
    far, near = pair(array, *FAR), pair(array, 2)
    if work:
        near, far, *work = lax.optimization_barrier((near, far, *work))
    return [far, pair(far, 1), near, array], work


def share_owner(share, member):
    own = lax.axis_index("src")
    odd = own % 2
    first, second = FAR[0] + (FAR[1] - FAR[0]) * odd, FAR[1] + (FAR[0] - FAR[1]) * odd
    return own ^ (first, second ^ 1, 2, 0)[share] ^ member


def shards(
    flows, speeds, seg_length, relay_list, seg_slot, tile_pairs, tile_count, attenuation, dwellings
):
    sources, receivers = lax.axis_size("src"), lax.axis_size("rcv")
    hours = flows.shape[0]
    slots = sources * WIDTH
    f32, i32, bf16 = jnp.float32, jnp.int32, jnp.bfloat16
    blocks, facades = seg_slot.shape[0] // LANES, dwellings.shape[0] // LANES
    hours_weight = sum(
        1.0 if 7 <= h < 19 else (ROOT if 19 <= h < 23 else 10.0) for h in range(hours)
    )

    def vmem(shape, dtype):
        return (shape, dtype, "vmem")

    pairwise = sources == 8
    copies = 1 if pairwise else sources
    (power,) = call(
        functools.partial(source_kernel, copies),
        "source",
        [vmem((copies * BANDS, LANES), f32)],
        [(flows, "hbm"), (speeds, "hbm")],
        [
            pltpu.VMEM((hours, LANES), f32),
            pltpu.VMEM((hours, LANES), f32),
            pltpu.SemaphoreType.DMA((2,)),
        ],
    )
    tables, spread, ints, floats, people, tiles, pairs = call(
        prepare_kernel,
        "prepare",
        [
            vmem((2 * BANDS, hours, LANES), f32),
            vmem((blocks * LANES, slots), bf16),
            vmem((sources + blocks, LANES), i32),
            vmem((sources + blocks, LANES), f32),
            vmem((facades, LANES), i32),
            vmem(attenuation.shape[2:], bf16),
            (tile_pairs.shape[2:], i32, "smem"),
        ],
        [
            (array, "hbm")
            for array in (
                tile_pairs[0, 0],
                flows,
                speeds,
                seg_slot.reshape(blocks, LANES),
                relay_list[0],
                seg_length.reshape(blocks, LANES),
                dwellings.reshape(facades, LANES),
                attenuation[0, 0],
            )
        ],
        [
            pltpu.VMEM((hours, LANES), f32),
            pltpu.VMEM((hours, LANES), f32),
            pltpu.VMEM((sources, WIDTH), i32),
            pltpu.VMEM((sources, LANES), i32),
            pltpu.SemaphoreType.DMA((8,)),
        ],
    )
    if pairwise:
        power = jnp.concatenate([power, pair(power, 1)], axis=0)
        powers, (ints,) = exchange(power, [ints])
    else:
        powers = [lax.all_to_all(power, "src", 0, 0, tiled=True)]
    here = [(pairs, "smem"), (tile_count, "")]
    (part,) = call(
        functools.partial(forward_kernel, pairwise, copies),
        "forward",
        [vmem((copies * facades, LANES), f32)],
        here + [(array, "vmem") for array in (ints, floats, tiles, *powers)],
        [
            pltpu.VMEM((blocks, 2 * BANDS, LANES), bf16),
            pltpu.VMEM((facades, 2 * BANDS, LANES), f32),
        ],
    )
    (turned,) = call(
        turn_kernel,
        "turn",
        [vmem(attenuation.shape[2:], bf16)],
        [(tile_count, ""), (tiles, "vmem"), (part, "vmem")],
    )
    if pairwise:
        other, turned = lax.optimization_barrier((pair(part, 1), turned))
        total = part + other
        parts, _ = exchange(total, [])
    else:
        parts = [lax.all_to_all(part, "src", 0, 0, tiled=True)]
    (back,) = call(
        functools.partial(backward_kernel, hours, hours_weight, receivers),
        "backward",
        [vmem((receivers * sources * ROWS, LANES), f32)],
        here + [(array, "vmem") for array in (people, floats, spread, turned, *parts)],
        [
            pltpu.VMEM((facades, 32, LANES), bf16),
            pltpu.VMEM((blocks, 32, LANES), f32),
        ],
    )
    back = back.reshape(receivers * sources, ROWS, LANES)
    back = lax.all_to_all(back, ("rcv", "src"), 0, 0, tiled=True)
    back = back.reshape(receivers * sources * ROWS, LANES)
    grad_flows, grad_speeds, annoyed = call(
        functools.partial(finish_kernel, receivers),
        "finish",
        [((hours, LANES), f32, ""), ((hours, LANES), f32, ""), ((1, LANES), f32, "")],
        [(array, "vmem") for array in (back, tables)],
    )
    return grad_flows, grad_speeds, annoyed[0, 0]


def solution(mesh):
    in_specs = (
        P(None, "src"),
        P(None, "src"),
        P("src"),
        P("src", None, None),
        P("src"),
        P("src", "rcv", None, None),
        P("src", "rcv"),
        P("src", "rcv", None, None, None, None),
        P("rcv"),
    )
    out_specs = (P(None, "src"), P(None, "src"), P())
    return jax.shard_map(shards, mesh=mesh, in_specs=in_specs, out_specs=out_specs, check_vma=False)
```

```python
import functools
import math

import jax
import jax.numpy as jnp
from jax import lax
from jax.experimental import pallas as pl
from jax.experimental.pallas import tpu as pltpu
from jax.sharding import PartitionSpec as P

rolling_base = [79.7, 85.7, 84.5, 90.2, 97.3, 93.9, 84.1, 74.3]
rolling_slope = [30.0, 41.5, 38.9, 25.7, 32.5, 37.2, 39.0, 40.0]
propel_base = [94.5, 89.2, 88.0, 85.9, 84.2, 86.9, 83.3, 76.1]
propel_slope = [-1.3, 7.2, 7.7, 8.0, 8.0, 8.0, 8.0, 8.0]
aweight_db = [-26.2, -16.1, -8.6, -3.2, 0.0, 1.2, 1.0, -1.1]

BANDS = 8
LANES = 128
CLASSES = 3
WIDTH = 16
VMEM_BYTES = 8 * 2**20
ROWS = 4
TOGETHER = 6
TURNED = 4
ROOT = math.sqrt(10.0)
DECIBEL = math.log(10.0) / 10.0
NT = (((1,), (1,)), ((), ()))


def iota(shape, axis):
    return lax.broadcasted_iota(jnp.int32, shape, axis)


def hour_class(shape):
    hour = iota(shape, 0)
    day = (hour >= 7) & (hour < 19)
    evening = (hour >= 19) & (hour < 23)
    return jnp.where(day, 0, jnp.where(evening, 1, 2))


def log10_ratio(speed_kmh):
    return jnp.log(speed_kmh / 70.0) * (1.0 / math.log(10.0))


def band_terms(speed_kmh, log_ratio):
    terms, propels = [], {}
    for band in range(BANDS):
        shift = aweight_db[band] - 90.0
        rolling = jnp.exp(
            DECIBEL * (rolling_base[band] + shift) + (DECIBEL * rolling_slope[band]) * log_ratio
        )
        slope = propel_slope[band]
        if slope not in propels:
            propels[slope] = jnp.exp((DECIBEL * slope / 70.0) * (speed_kmh - 70.0))
        terms.append((rolling, math.exp(DECIBEL * (propel_base[band] + shift)) * propels[slope]))
    return terms


def lane_pick(table, index):
    return jnp.take_along_axis(table, index, axis=1, mode="promise_in_bounds")


def swap_groups(block):
    row, lane = iota((8, LANES), 0), iota((8, LANES), 1)
    block = lane_pick(block, (lane + LANES - WIDTH * row) % LANES)
    block = jnp.take_along_axis(
        block, (lane // WIDTH + 8 - row) % 8, axis=0, mode="promise_in_bounds"
    )
    return lane_pick(block, (lane + WIDTH * row) % LANES)


def each_tile(pairs_ref, count, read, multiply, write, acc_ref):
    def step(turn, carry):
        added = []
        for place in range(TOGETHER):
            number = turn * TOGETHER + place
            tile = jnp.minimum(number, count - 1)
            value = read(tile)
            value = jnp.where(number < count, value, jnp.zeros_like(value))
            added.append((write(tile), multiply(value, tile)))
        for block, value in added:
            acc_ref[block] += value
        return carry

    lax.fori_loop(0, (count + TOGETHER - 1) // TOGETHER, step, 0)


def stack_sums(blocks):
    row = iota((8, LANES), 0)
    for distance in (4, 2, 1):
        half = len(blocks) // 2
        near = (row & distance) == 0
        blocks = [
            jnp.where(near, first, second)
            + jnp.take_along_axis(
                jnp.where(near, second, first), row ^ distance, axis=0, mode="promise_in_bounds"
            )
            for first, second in zip(blocks[:half], blocks[half:])
        ]
    return blocks[0]


def only_band(value, band):
    row = iota(value.shape, 0) % BANDS
    return jnp.where(row == band, value, jnp.zeros_like(value))


def split2(value):
    high = value.astype(jnp.bfloat16)
    low = (value - high.astype(jnp.float32)).astype(jnp.bfloat16)
    return high, low


def source_kernel(copies, flow_hbm, speed_hbm, out_ref, flow_ref, speed_ref, sems):
    fetches = [
        pltpu.make_async_copy(speed_hbm, speed_ref, sems.at[0]),
        pltpu.make_async_copy(flow_hbm, flow_ref, sems.at[1]),
    ]
    for fetch in fetches:
        fetch.start()
    fetches[0].wait()
    speed = speed_ref[...]
    speed_kmh = 100.0 * speed
    log_ratio = log10_ratio(speed_kmh)
    terms = band_terms(speed_kmh, log_ratio)
    kind = hour_class(speed.shape)
    weight = jnp.where(kind == 0, 1.0, jnp.where(kind == 1, ROOT, 10.0)) / speed_kmh
    fetches[1].wait()
    scale = weight * flow_ref[...]
    sums = []
    for rolling, propel in terms:
        power = scale * (rolling + propel)
        sums.append(sum(power[k : k + 8] for k in range(8, power.shape[0], 8)) + power[:8])
    result = stack_sums(sums)
    for copy in range(copies):
        out_ref[copy * BANDS : (copy + 1) * BANDS] = result


def prepare_kernel(
    pairs_hbm, flow_hbm, speed_hbm, slot_hbm, relay_hbm, length_hbm, people_hbm, tile_hbm,
    table_ref, spread_ref, ints_ref, floats_ref, people_ref, tile_ref, pairs_ref, flow_ref, speed_ref, relay_ref, relay_scratch, sems,
):
    owners, blocks = relay_hbm.shape[0], slot_hbm.shape[0]
    index_ref, slot_ref = ints_ref.at[:owners], ints_ref.at[owners:]
    wide_ref, length_ref = floats_ref.at[:owners], floats_ref.at[owners:]
    moves = [
        (flow_hbm, flow_ref),
        (speed_hbm, speed_ref),
        (relay_hbm, relay_ref),
        (slot_hbm, slot_ref),
        (pairs_hbm, pairs_ref),
        (length_hbm, length_ref),
        (people_hbm, people_ref),
        (tile_hbm, tile_ref),
    ]
    fetches = [
        pltpu.make_async_copy(start, end, sems.at[k]) for k, (start, end) in enumerate(moves)
    ]
    for fetch in fetches:
        fetch.start()
    for fetch in fetches[:4]:
        fetch.wait()
    relay_scratch[...] = jnp.zeros(relay_scratch.shape, jnp.int32)
    relay_scratch[:, :WIDTH] = relay_ref[...]
    lane, row = iota((8, LANES), 1), iota((8, LANES), 0)
    for group in range(owners // 8):
        rows = slice(group * 8, group * 8 + 8)
        wide = lane_pick(relay_scratch[rows], lane % WIDTH)
        wide_ref[rows] = wide.astype(jnp.float32)
        picked = jnp.where(lane // WIDTH == row, jnp.maximum(wide, 0), 0)
        picked = jnp.sum(picked, axis=0, keepdims=True)
        index_ref[rows] = jnp.broadcast_to(picked, (8, LANES))
    flow, speed = flow_ref[...], speed_ref[...]
    speed_kmh = 100.0 * speed
    terms = band_terms(speed_kmh, log10_ratio(speed_kmh))
    per_flow = 1.0 / speed_kmh
    factor = flow * per_flow
    inverse = 1.0 / speed
    for band, (rolling, propel) in enumerate(terms):
        table_ref[band] = per_flow * (rolling + propel)
        table_ref[BANDS + band] = factor * (
            rolling * (rolling_slope[band] / 10.0 - 1.0) * inverse
            + propel * (math.log(10.0) * propel_slope[band] / 7.0 - inverse)
        )
    slots = spread_ref.shape[1]
    for block in range(blocks):
        same = iota((slots, LANES), 0) == slot_ref[block : block + 1]
        spread_ref[block * LANES : (block + 1) * LANES] = (
            jnp.where(same, 1.0, 0.0).T.astype(jnp.bfloat16)
        )
    for fetch in fetches[4:]:
        fetch.wait()


def turn_kernel(count_ref, tile_ref, part_ref, out_ref):
    count = count_ref[0, 0]

    def step(turn, carry):
        for place in range(TURNED):
            tile = jnp.minimum(turn * TURNED + place, count - 1)
            for band in range(BANDS):
                out_ref[tile, band] = tile_ref[tile, band].T
        return carry

    lax.fori_loop(0, (count + TURNED - 1) // TURNED, step, 0)


def forward_kernel(shared, copies, pairs_ref, count_ref, ints_ref, floats_ref, tile_ref, *refs):
    link_refs, (out_ref, seg_scratch, acc_scratch) = refs[:-3], refs[-3:]
    each = link_refs[0].shape[0] // BANDS
    owners = each * len(link_refs)
    groups = owners // 8
    index_ref, slot_ref, length_ref = ints_ref, ints_ref.at[owners:], floats_ref.at[owners:]
    place = iota((BANDS, LANES), 1) // WIDTH
    tables = []
    for group in range(groups):
        index = index_ref[group * 8 : group * 8 + 8]
        table = jnp.zeros((BANDS, LANES), jnp.float32)
        for member in range(8):
            block = group * 8 + member
            rows = slice(block % each * BANDS, (block % each + 1) * BANDS)
            picked = lane_pick(link_refs[block // each][rows], index)
            if shared:
                member = share_owner(block // each, block % each)
            table = jnp.where(place == member, picked, table)
        tables.append(table)
    blocks = slot_ref.shape[0]
    for block in range(blocks):
        slot = jnp.broadcast_to(slot_ref[block : block + 1], (BANDS, LANES))
        value = lane_pick(tables[0], slot % LANES)
        for group in range(1, groups):
            value = jnp.where(slot // LANES == group, lane_pick(tables[group], slot % LANES), value)
        high, low = split2(value * length_ref[block : block + 1])
        seg_scratch[block] = jnp.concatenate([high, low], axis=0)
    acc_scratch[...] = jnp.zeros(acc_scratch.shape, jnp.float32)

    def multiply(seg, tile):
        rows = jnp.concatenate([only_band(seg, band) for band in range(BANDS)], axis=1)
        tiles = tile_ref[tile].reshape(BANDS * LANES, LANES)
        return jnp.dot(rows, tiles, preferred_element_type=jnp.float32)

    each_tile(
        pairs_ref,
        count_ref[0, 0],
        lambda tile: seg_scratch[pairs_ref[0, tile]],
        multiply,
        lambda tile: pairs_ref[1, tile],
        acc_scratch,
    )
    facades = acc_scratch.shape[0]
    result = stack_sums([acc_scratch[block, :8] + acc_scratch[block, 8:] for block in range(facades)])
    for copy in range(copies):
        out_ref[copy * facades : (copy + 1) * facades] = result


def backward_kernel(
    hours, hours_weight, receivers, pairs_ref, count_ref, people_ref, floats_ref, spread_ref, tile_ref, *refs
):
    part_refs, (out_ref, grad_scratch, acc_scratch) = refs[:-3], refs[-3:]
    facades = people_ref.shape[0]
    owners = out_ref.shape[0] // (receivers * ROWS)
    relay_ref, length_ref = floats_ref, floats_ref.at[owners:]
    parts = [
        ref[first : first + facades]
        for ref in part_refs
        for first in range(0, ref.shape[0], facades)
    ]
    while len(parts) > 1:
        parts = [sum(parts[k + 1 : k + 2], parts[k]) for k in range(0, len(parts), 2)]
    (total,) = parts
    total = total + 0.01 * hours_weight
    level = (60.0 - 10.0 * math.log10(hours)) + (10.0 / math.log(10.0)) * jnp.log(total)
    people = people_ref[...].astype(jnp.float32)
    rise = (0.1 / math.log(10.0)) * people * (-3.1162 + 0.0684 * level)
    slope = rise / total
    grads = [slope, slope * ROOT, slope * 10.0]
    pad = jnp.zeros((8, LANES), jnp.float32)
    for block in range(facades):
        rows = [jnp.broadcast_to(g[block : block + 1], (BANDS, LANES)) for g in grads]
        grad_scratch[block] = jnp.concatenate(rows + [pad], axis=0).astype(jnp.bfloat16)
    acc_scratch[...] = jnp.zeros(acc_scratch.shape, jnp.float32)

    def multiply(grad, tile):
        rows = jnp.concatenate([only_band(grad, band) for band in range(BANDS)], axis=1)
        tiles = tile_ref[tile].reshape(BANDS * LANES, LANES)
        return jnp.dot(rows, tiles, preferred_element_type=jnp.float32)

    each_tile(
        pairs_ref,
        count_ref[0, 0],
        lambda tile: grad_scratch[pairs_ref[1, tile]],
        multiply,
        lambda tile: pairs_ref[0, tile],
        acc_scratch,
    )
    annoyed = (0.01 * people) * (78.927 - 3.1162 * level + 0.0342 * level * level)
    annoyed = jnp.sum(annoyed, keepdims=True)
    used = CLASSES * BANDS
    blocks = acc_scratch.shape[0]
    high, low = [], []
    for block in range(blocks):
        value = acc_scratch[block][:used] * length_ref[block : block + 1]
        high_part = value.astype(jnp.bfloat16).astype(jnp.float32)
        high.append(high_part)
        low.append(value - high_part)
    rows = jnp.concatenate(
        [jnp.concatenate(high, axis=1), jnp.concatenate(low, axis=1)], axis=0
    ).astype(jnp.bfloat16)
    slots = jnp.dot(rows, spread_ref[...], preferred_element_type=jnp.float32)
    slots = slots[:used] + slots[used:]
    place = iota((8, LANES), 1) // WIDTH
    for group in range(owners // 8):
        lanes = slice(group * LANES, (group + 1) * LANES)
        rows = [
            swap_groups(slots[kind * BANDS : (kind + 1) * BANDS, lanes])
            for kind in range(CLASSES)
        ]
        rows.append(jnp.where(place == 0, relay_ref[group * 8 : group * 8 + 8], annoyed))
        for receiver in range(receivers):
            first = (receiver * owners + group * 8) * ROWS
            for kind in range(ROWS):
                out_ref[pl.ds(first + kind, 8, stride=ROWS), :] = rows[kind]


def finish_kernel(receivers, in_ref, table_ref, flow_out, speed_out, count_out):
    owners = in_ref.shape[0] // (receivers * ROWS)
    place, row = iota((8, LANES), 1) // WIDTH, iota((8, LANES), 0)
    used = CLASSES * BANDS
    links = jnp.zeros((2 * used, LANES), jnp.float32)
    for group in range(owners // 8):
        parts = []
        for kind in range(ROWS):
            rows = [
                in_ref[pl.ds((receiver * owners + group * 8) * ROWS + kind, 8, stride=ROWS), :]
                for receiver in range(receivers)
            ]
            total = sum(rows[1:], rows[0])
            parts.append(swap_groups(total) if kind < CLASSES else rows[0])
        if group == 0:
            count_out[...] = jnp.broadcast_to(total[0:1, LANES - 1 :], (1, LANES))
        value = jnp.concatenate(parts[:CLASSES], axis=0)
        high = value.astype(jnp.bfloat16).astype(jnp.float32)
        rows = jnp.concatenate([high, value - high], axis=0).astype(jnp.bfloat16)
        relay = lane_pick(parts[CLASSES], iota((8, LANES), 1) % WIDTH)
        relay = jnp.sum(jnp.where(place == row, relay, 0.0), axis=0, keepdims=True)
        relay = relay.astype(jnp.int32)
        spread = jnp.where(iota((LANES, LANES), 0) == relay, 1.0, 0.0).astype(jnp.bfloat16)
        links = links + lax.dot_general(rows, spread, NT, preferred_element_type=jnp.float32)
    links = links[:used] + links[used:]
    kind = hour_class(flow_out.shape)
    flow_sum = jnp.zeros(flow_out.shape, jnp.float32)
    speed_sum = jnp.zeros(flow_out.shape, jnp.float32)
    for band in range(BANDS):
        day, evening, night = [
            links[k * BANDS + band : k * BANDS + band + 1] for k in range(CLASSES)
        ]
        back = jnp.where(kind == 0, day, jnp.where(kind == 1, evening, night))
        flow_sum = flow_sum + back * table_ref[band]
        speed_sum = speed_sum + back * table_ref[BANDS + band]
    flow_out[...] = flow_sum
    speed_out[...] = speed_sum


def call(kernel, name, outs, args, scratch=()):
    space = {"smem": pltpu.SMEM, "vmem": pltpu.VMEM, "hbm": pltpu.HBM}
    return pl.pallas_call(
        kernel,
        out_shape=[
            space[place](shape, dtype) if place else jax.ShapeDtypeStruct(shape, dtype)
            for shape, dtype, place in outs
        ],
        in_specs=[pl.BlockSpec(memory_space=space[place or "smem"]) for _, place in args],
        out_specs=[pl.BlockSpec(memory_space=space[place or "vmem"]) for _, _, place in outs],
        scratch_shapes=list(scratch),
        compiler_params=pltpu.CompilerParams(vmem_limit_bytes=VMEM_BYTES),
        name=name,
    )(
        *[
            pltpu.with_memory_space_constraint(array, space[place]) if place else array
            for array, place in args
        ]
    )


def pair(array, *distances):
    sources = lax.axis_size("src")
    return lax.ppermute(
        array, "src", [(k, k ^ distances[k % len(distances)]) for k in range(sources)]
    )


FAR = (4, 6)


def exchange(array, work):
    far, near = pair(array, *FAR), pair(array, 2)
    if work:
        near, far, *work = lax.optimization_barrier((near, far, *work))
    return [far, pair(far, 1), near, array], work


def share_owner(share, member):
    own = lax.axis_index("src")
    odd = own % 2
    first, second = FAR[0] + (FAR[1] - FAR[0]) * odd, FAR[1] + (FAR[0] - FAR[1]) * odd
    return own ^ (first, second ^ 1, 2, 0)[share] ^ member


def shards(
    flows, speeds, seg_length, relay_list, seg_slot, tile_pairs, tile_count, attenuation, dwellings
):
    sources, receivers = lax.axis_size("src"), lax.axis_size("rcv")
    hours = flows.shape[0]
    slots = sources * WIDTH
    f32, i32, bf16 = jnp.float32, jnp.int32, jnp.bfloat16
    blocks, facades = seg_slot.shape[0] // LANES, dwellings.shape[0] // LANES
    hours_weight = sum(
        1.0 if 7 <= h < 19 else (ROOT if 19 <= h < 23 else 10.0) for h in range(hours)
    )

    def vmem(shape, dtype):
        return (shape, dtype, "vmem")

    pairwise = sources == 8
    copies = 1 if pairwise else sources
    (power,) = call(
        functools.partial(source_kernel, copies),
        "source",
        [vmem((copies * BANDS, LANES), f32)],
        [(flows, "hbm"), (speeds, "hbm")],
        [
            pltpu.VMEM((hours, LANES), f32),
            pltpu.VMEM((hours, LANES), f32),
            pltpu.SemaphoreType.DMA((2,)),
        ],
    )
    tables, spread, ints, floats, people, tiles, pairs = call(
        prepare_kernel,
        "prepare",
        [
            vmem((2 * BANDS, hours, LANES), f32),
            vmem((blocks * LANES, slots), bf16),
            vmem((sources + blocks, LANES), i32),
            vmem((sources + blocks, LANES), f32),
            vmem((facades, LANES), i32),
            vmem(attenuation.shape[2:], bf16),
            (tile_pairs.shape[2:], i32, "smem"),
        ],
        [
            (array, "hbm")
            for array in (
                tile_pairs[0, 0],
                flows,
                speeds,
                seg_slot.reshape(blocks, LANES),
                relay_list[0],
                seg_length.reshape(blocks, LANES),
                dwellings.reshape(facades, LANES),
                attenuation[0, 0],
            )
        ],
        [
            pltpu.VMEM((hours, LANES), f32),
            pltpu.VMEM((hours, LANES), f32),
            pltpu.VMEM((sources, WIDTH), i32),
            pltpu.VMEM((sources, LANES), i32),
            pltpu.SemaphoreType.DMA((8,)),
        ],
    )
    if pairwise:
        power = jnp.concatenate([power, pair(power, 1)], axis=0)
        powers, (ints,) = exchange(power, [ints])
    else:
        powers = [lax.all_to_all(power, "src", 0, 0, tiled=True)]
    here = [(pairs, "smem"), (tile_count, "")]
    (part,) = call(
        functools.partial(forward_kernel, pairwise, copies),
        "forward",
        [vmem((copies * facades, LANES), f32)],
        here + [(array, "vmem") for array in (ints, floats, tiles, *powers)],
        [
            pltpu.VMEM((blocks, 2 * BANDS, LANES), bf16),
            pltpu.VMEM((facades, 2 * BANDS, LANES), f32),
        ],
    )
    (turned,) = call(
        turn_kernel,
        "turn",
        [vmem(attenuation.shape[2:], bf16)],
        [(tile_count, ""), (tiles, "vmem"), (part, "vmem")],
    )
    if pairwise:
        other, turned = lax.optimization_barrier((pair(part, 1), turned))
        total = part + other
        parts, _ = exchange(total, [])
    else:
        parts = [lax.all_to_all(part, "src", 0, 0, tiled=True)]
    (back,) = call(
        functools.partial(backward_kernel, hours, hours_weight, receivers),
        "backward",
        [vmem((receivers * sources * ROWS, LANES), f32)],
        here + [(array, "vmem") for array in (people, floats, spread, turned, *parts)],
        [
            pltpu.VMEM((facades, 32, LANES), bf16),
            pltpu.VMEM((blocks, 32, LANES), f32),
        ],
    )
    back = back.reshape(receivers * sources, ROWS, LANES)
    back = lax.all_to_all(back, ("rcv", "src"), 0, 0, tiled=True)
    back = back.reshape(receivers * sources * ROWS, LANES)
    grad_flows, grad_speeds, annoyed = call(
        functools.partial(finish_kernel, receivers),
        "finish",
        [((hours, LANES), f32, ""), ((hours, LANES), f32, ""), ((1, LANES), f32, "")],
        [(array, "vmem") for array in (back, tables)],
    )
    return grad_flows, grad_speeds, annoyed[0, 0]


def solution(mesh):
    in_specs = (
        P(None, "src"),
        P(None, "src"),
        P("src"),
        P("src", None, None),
        P("src"),
        P("src", "rcv", None, None),
        P("src", "rcv"),
        P("src", "rcv", None, None, None, None),
        P("rcv"),
    )
    out_specs = (P(None, "src"), P(None, "src"), P())
    return jax.shard_map(shards, mesh=mesh, in_specs=in_specs, out_specs=out_specs, check_vma=False)
```

```python
import functools
import math

import jax
import jax.numpy as jnp
from jax import lax
from jax.experimental import pallas as pl
from jax.experimental.pallas import tpu as pltpu
from jax.sharding import PartitionSpec as P

rolling_base = [79.7, 85.7, 84.5, 90.2, 97.3, 93.9, 84.1, 74.3]
rolling_slope = [30.0, 41.5, 38.9, 25.7, 32.5, 37.2, 39.0, 40.0]
propel_base = [94.5, 89.2, 88.0, 85.9, 84.2, 86.9, 83.3, 76.1]
propel_slope = [-1.3, 7.2, 7.7, 8.0, 8.0, 8.0, 8.0, 8.0]
aweight_db = [-26.2, -16.1, -8.6, -3.2, 0.0, 1.2, 1.0, -1.1]

BANDS = 8
LANES = 128
CLASSES = 3
WIDTH = 16
VMEM_BYTES = 8 * 2**20
ROWS = 4
TOGETHER = 6
TURNED = 3
ROOT = math.sqrt(10.0)
DECIBEL = math.log(10.0) / 10.0
NT = (((1,), (1,)), ((), ()))


def iota(shape, axis):
    return lax.broadcasted_iota(jnp.int32, shape, axis)


def hour_class(shape):
    hour = iota(shape, 0)
    day = (hour >= 7) & (hour < 19)
    evening = (hour >= 19) & (hour < 23)
    return jnp.where(day, 0, jnp.where(evening, 1, 2))


def log10_ratio(speed_kmh):
    return jnp.log(speed_kmh / 70.0) * (1.0 / math.log(10.0))


def band_terms(speed_kmh, log_ratio):
    terms, propels = [], {}
    for band in range(BANDS):
        shift = aweight_db[band] - 90.0
        rolling = jnp.exp(
            DECIBEL * (rolling_base[band] + shift) + (DECIBEL * rolling_slope[band]) * log_ratio
        )
        slope = propel_slope[band]
        if slope not in propels:
            propels[slope] = jnp.exp((DECIBEL * slope / 70.0) * (speed_kmh - 70.0))
        terms.append((rolling, math.exp(DECIBEL * (propel_base[band] + shift)) * propels[slope]))
    return terms


def lane_pick(table, index):
    return jnp.take_along_axis(table, index, axis=1, mode="promise_in_bounds")


def swap_groups(block):
    row, lane = iota((8, LANES), 0), iota((8, LANES), 1)
    block = lane_pick(block, (lane + LANES - WIDTH * row) % LANES)
    block = jnp.take_along_axis(
        block, (lane // WIDTH + 8 - row) % 8, axis=0, mode="promise_in_bounds"
    )
    return lane_pick(block, (lane + WIDTH * row) % LANES)


def each_tile(pairs_ref, count, read, multiply, write, acc_ref):
    def step(turn, carry):
        added = []
        for place in range(TOGETHER):
            number = turn * TOGETHER + place
            tile = jnp.minimum(number, count - 1)
            value = read(tile)
            value = jnp.where(number < count, value, jnp.zeros_like(value))
            added.append((write(tile), multiply(value, tile)))
        for block, value in added:
            acc_ref[block] += value
        return carry

    lax.fori_loop(0, (count + TOGETHER - 1) // TOGETHER, step, 0)


def stack_sums(blocks):
    row = iota((8, LANES), 0)
    for distance in (4, 2, 1):
        half = len(blocks) // 2
        near = (row & distance) == 0
        blocks = [
            jnp.where(near, first, second)
            + jnp.take_along_axis(
                jnp.where(near, second, first), row ^ distance, axis=0, mode="promise_in_bounds"
            )
            for first, second in zip(blocks[:half], blocks[half:])
        ]
    return blocks[0]


def only_band(value, band):
    row = iota(value.shape, 0) % BANDS
    return jnp.where(row == band, value, jnp.zeros_like(value))


def split2(value):
    high = value.astype(jnp.bfloat16)
    low = (value - high.astype(jnp.float32)).astype(jnp.bfloat16)
    return high, low


def source_kernel(copies, flow_hbm, speed_hbm, out_ref, flow_ref, speed_ref, sems):
    fetches = [
        pltpu.make_async_copy(speed_hbm, speed_ref, sems.at[0]),
        pltpu.make_async_copy(flow_hbm, flow_ref, sems.at[1]),
    ]
    for fetch in fetches:
        fetch.start()
    fetches[0].wait()
    speed = speed_ref[...]
    speed_kmh = 100.0 * speed
    log_ratio = log10_ratio(speed_kmh)
    terms = band_terms(speed_kmh, log_ratio)
    kind = hour_class(speed.shape)
    weight = jnp.where(kind == 0, 1.0, jnp.where(kind == 1, ROOT, 10.0)) / speed_kmh
    fetches[1].wait()
    scale = weight * flow_ref[...]
    sums = []
    for rolling, propel in terms:
        power = scale * (rolling + propel)
        sums.append(sum(power[k : k + 8] for k in range(8, power.shape[0], 8)) + power[:8])
    result = stack_sums(sums)
    for copy in range(copies):
        out_ref[copy * BANDS : (copy + 1) * BANDS] = result


def prepare_kernel(
    pairs_hbm, flow_hbm, speed_hbm, slot_hbm, relay_hbm, length_hbm, people_hbm, tile_hbm,
    table_ref, spread_ref, ints_ref, floats_ref, people_ref, tile_ref, pairs_ref, flow_ref, speed_ref, relay_ref, relay_scratch, sems,
):
    owners, blocks = relay_hbm.shape[0], slot_hbm.shape[0]
    index_ref, slot_ref = ints_ref.at[:owners], ints_ref.at[owners:]
    wide_ref, length_ref = floats_ref.at[:owners], floats_ref.at[owners:]
    moves = [
        (flow_hbm, flow_ref),
        (speed_hbm, speed_ref),
        (relay_hbm, relay_ref),
        (slot_hbm, slot_ref),
        (pairs_hbm, pairs_ref),
        (length_hbm, length_ref),
        (people_hbm, people_ref),
        (tile_hbm, tile_ref),
    ]
    fetches = [
        pltpu.make_async_copy(start, end, sems.at[k]) for k, (start, end) in enumerate(moves)
    ]
    for fetch in fetches[:4] + fetches[-1:] + fetches[4:-1]:
        fetch.start()
    for fetch in fetches[:4]:
        fetch.wait()
    relay_scratch[...] = jnp.zeros(relay_scratch.shape, jnp.int32)
    relay_scratch[:, :WIDTH] = relay_ref[...]
    lane, row = iota((8, LANES), 1), iota((8, LANES), 0)
    for group in range(owners // 8):
        rows = slice(group * 8, group * 8 + 8)
        wide = lane_pick(relay_scratch[rows], lane % WIDTH)
        wide_ref[rows] = wide.astype(jnp.float32)
        picked = jnp.where(lane // WIDTH == row, jnp.maximum(wide, 0), 0)
        picked = jnp.sum(picked, axis=0, keepdims=True)
        index_ref[rows] = jnp.broadcast_to(picked, (8, LANES))
    flow, speed = flow_ref[...], speed_ref[...]
    speed_kmh = 100.0 * speed
    terms = band_terms(speed_kmh, log10_ratio(speed_kmh))
    per_flow = 1.0 / speed_kmh
    factor = flow * per_flow
    inverse = 1.0 / speed
    for band, (rolling, propel) in enumerate(terms):
        table_ref[band] = per_flow * (rolling + propel)
        table_ref[BANDS + band] = factor * (
            rolling * (rolling_slope[band] / 10.0 - 1.0) * inverse
            + propel * (math.log(10.0) * propel_slope[band] / 7.0 - inverse)
        )
    slots = spread_ref.shape[1]
    for block in range(blocks):
        same = iota((slots, LANES), 0) == slot_ref[block : block + 1]
        spread_ref[block * LANES : (block + 1) * LANES] = (
            jnp.where(same, 1.0, 0.0).T.astype(jnp.bfloat16)
        )
    for fetch in fetches[4:]:
        fetch.wait()


def turn_kernel(count_ref, tile_ref, part_ref, out_ref):
    count = count_ref[0, 0]

    def step(turn, carry):
        for place in range(TURNED):
            tile = jnp.minimum(turn * TURNED + place, count - 1)
            for band in range(BANDS):
                out_ref[tile, band] = tile_ref[tile, band].T
        return carry

    lax.fori_loop(0, (count + TURNED - 1) // TURNED, step, 0)


def forward_kernel(shared, copies, pairs_ref, count_ref, ints_ref, floats_ref, tile_ref, *refs):
    link_refs, (out_ref, seg_scratch, acc_scratch) = refs[:-3], refs[-3:]
    each = link_refs[0].shape[0] // BANDS
    owners = each * len(link_refs)
    groups = owners // 8
    index_ref, slot_ref, length_ref = ints_ref, ints_ref.at[owners:], floats_ref.at[owners:]
    place = iota((BANDS, LANES), 1) // WIDTH
    tables = []
    for group in range(groups):
        index = index_ref[group * 8 : group * 8 + 8]
        table = jnp.zeros((BANDS, LANES), jnp.float32)
        for member in range(8):
            block = group * 8 + member
            rows = slice(block % each * BANDS, (block % each + 1) * BANDS)
            picked = lane_pick(link_refs[block // each][rows], index)
            if shared:
                member = share_owner(block // each, block % each)
            table = jnp.where(place == member, picked, table)
        tables.append(table)
    blocks = slot_ref.shape[0]
    for block in range(blocks):
        slot = jnp.broadcast_to(slot_ref[block : block + 1], (BANDS, LANES))
        value = lane_pick(tables[0], slot % LANES)
        for group in range(1, groups):
            value = jnp.where(slot // LANES == group, lane_pick(tables[group], slot % LANES), value)
        high, low = split2(value * length_ref[block : block + 1])
        seg_scratch[block] = jnp.concatenate([high, low], axis=0)
    acc_scratch[...] = jnp.zeros(acc_scratch.shape, jnp.float32)

    def multiply(seg, tile):
        rows = jnp.concatenate([only_band(seg, band) for band in range(BANDS)], axis=1)
        tiles = tile_ref[tile].reshape(BANDS * LANES, LANES)
        return jnp.dot(rows, tiles, preferred_element_type=jnp.float32)

    each_tile(
        pairs_ref,
        count_ref[0, 0],
        lambda tile: seg_scratch[pairs_ref[0, tile]],
        multiply,
        lambda tile: pairs_ref[1, tile],
        acc_scratch,
    )
    facades = acc_scratch.shape[0]
    result = stack_sums([acc_scratch[block, :8] + acc_scratch[block, 8:] for block in range(facades)])
    for copy in range(copies):
        out_ref[copy * facades : (copy + 1) * facades] = result


def backward_kernel(
    hours, hours_weight, receivers, pairs_ref, count_ref, people_ref, floats_ref, spread_ref, tile_ref, *refs
):
    part_refs, (out_ref, grad_scratch, acc_scratch) = refs[:-3], refs[-3:]
    facades = people_ref.shape[0]
    owners = out_ref.shape[0] // (receivers * ROWS)
    relay_ref, length_ref = floats_ref, floats_ref.at[owners:]
    parts = [
        ref[first : first + facades]
        for ref in part_refs
        for first in range(0, ref.shape[0], facades)
    ]
    while len(parts) > 1:
        parts = [sum(parts[k + 1 : k + 2], parts[k]) for k in range(0, len(parts), 2)]
    (total,) = parts
    total = total + 0.01 * hours_weight
    level = (60.0 - 10.0 * math.log10(hours)) + (10.0 / math.log(10.0)) * jnp.log(total)
    people = people_ref[...].astype(jnp.float32)
    rise = (0.1 / math.log(10.0)) * people * (-3.1162 + 0.0684 * level)
    slope = rise / total
    grads = [slope, slope * ROOT, slope * 10.0]
    pad = jnp.zeros((8, LANES), jnp.float32)
    for block in range(facades):
        rows = [jnp.broadcast_to(g[block : block + 1], (BANDS, LANES)) for g in grads]
        grad_scratch[block] = jnp.concatenate(rows + [pad], axis=0).astype(jnp.bfloat16)
    acc_scratch[...] = jnp.zeros(acc_scratch.shape, jnp.float32)

    def multiply(grad, tile):
        rows = jnp.concatenate([only_band(grad, band) for band in range(BANDS)], axis=1)
        tiles = tile_ref[tile].reshape(BANDS * LANES, LANES)
        return jnp.dot(rows, tiles, preferred_element_type=jnp.float32)

    each_tile(
        pairs_ref,
        count_ref[0, 0],
        lambda tile: grad_scratch[pairs_ref[1, tile]],
        multiply,
        lambda tile: pairs_ref[0, tile],
        acc_scratch,
    )
    annoyed = (0.01 * people) * (78.927 - 3.1162 * level + 0.0342 * level * level)
    annoyed = jnp.sum(annoyed, keepdims=True)
    used = CLASSES * BANDS
    blocks = acc_scratch.shape[0]
    high, low = [], []
    for block in range(blocks):
        value = acc_scratch[block][:used] * length_ref[block : block + 1]
        high_part = value.astype(jnp.bfloat16).astype(jnp.float32)
        high.append(high_part)
        low.append(value - high_part)
    rows = jnp.concatenate(
        [jnp.concatenate(high, axis=1), jnp.concatenate(low, axis=1)], axis=0
    ).astype(jnp.bfloat16)
    slots = jnp.dot(rows, spread_ref[...], preferred_element_type=jnp.float32)
    slots = slots[:used] + slots[used:]
    place = iota((8, LANES), 1) // WIDTH
    for group in range(owners // 8):
        lanes = slice(group * LANES, (group + 1) * LANES)
        rows = [
            swap_groups(slots[kind * BANDS : (kind + 1) * BANDS, lanes])
            for kind in range(CLASSES)
        ]
        rows.append(jnp.where(place == 0, relay_ref[group * 8 : group * 8 + 8], annoyed))
        for receiver in range(receivers):
            first = (receiver * owners + group * 8) * ROWS
            for kind in range(ROWS):
                out_ref[pl.ds(first + kind, 8, stride=ROWS), :] = rows[kind]


def finish_kernel(receivers, in_ref, table_ref, flow_out, speed_out, count_out):
    owners = in_ref.shape[0] // (receivers * ROWS)
    place, row = iota((8, LANES), 1) // WIDTH, iota((8, LANES), 0)
    used = CLASSES * BANDS
    links = jnp.zeros((2 * used, LANES), jnp.float32)
    for group in range(owners // 8):
        parts = []
        for kind in range(ROWS):
            rows = [
                in_ref[pl.ds((receiver * owners + group * 8) * ROWS + kind, 8, stride=ROWS), :]
                for receiver in range(receivers)
            ]
            total = sum(rows[1:], rows[0])
            parts.append(swap_groups(total) if kind < CLASSES else rows[0])
        if group == 0:
            count_out[...] = jnp.broadcast_to(total[0:1, LANES - 1 :], (1, LANES))
        value = jnp.concatenate(parts[:CLASSES], axis=0)
        high = value.astype(jnp.bfloat16).astype(jnp.float32)
        rows = jnp.concatenate([high, value - high], axis=0).astype(jnp.bfloat16)
        relay = lane_pick(parts[CLASSES], iota((8, LANES), 1) % WIDTH)
        relay = jnp.sum(jnp.where(place == row, relay, 0.0), axis=0, keepdims=True)
        relay = relay.astype(jnp.int32)
        spread = jnp.where(iota((LANES, LANES), 0) == relay, 1.0, 0.0).astype(jnp.bfloat16)
        links = links + lax.dot_general(rows, spread, NT, preferred_element_type=jnp.float32)
    links = links[:used] + links[used:]
    kind = hour_class(flow_out.shape)
    flow_sum = jnp.zeros(flow_out.shape, jnp.float32)
    speed_sum = jnp.zeros(flow_out.shape, jnp.float32)
    for band in range(BANDS):
        day, evening, night = [
            links[k * BANDS + band : k * BANDS + band + 1] for k in range(CLASSES)
        ]
        back = jnp.where(kind == 0, day, jnp.where(kind == 1, evening, night))
        flow_sum = flow_sum + back * table_ref[band]
        speed_sum = speed_sum + back * table_ref[BANDS + band]
    flow_out[...] = flow_sum
    speed_out[...] = speed_sum


def call(kernel, name, outs, args, scratch=()):
    space = {"smem": pltpu.SMEM, "vmem": pltpu.VMEM, "hbm": pltpu.HBM}
    return pl.pallas_call(
        kernel,
        out_shape=[
            space[place](shape, dtype) if place else jax.ShapeDtypeStruct(shape, dtype)
            for shape, dtype, place in outs
        ],
        in_specs=[pl.BlockSpec(memory_space=space[place or "smem"]) for _, place in args],
        out_specs=[pl.BlockSpec(memory_space=space[place or "vmem"]) for _, _, place in outs],
        scratch_shapes=list(scratch),
        compiler_params=pltpu.CompilerParams(vmem_limit_bytes=VMEM_BYTES),
        name=name,
    )(
        *[
            pltpu.with_memory_space_constraint(array, space[place]) if place else array
            for array, place in args
        ]
    )


def pair(array, *distances):
    sources = lax.axis_size("src")
    return lax.ppermute(
        array, "src", [(k, k ^ distances[k % len(distances)]) for k in range(sources)]
    )


FAR = (4, 6)


def exchange(array, work):
    far, near = pair(array, *FAR), pair(array, 2)
    if work:
        near, far, *work = lax.optimization_barrier((near, far, *work))
    return [far, pair(far, 1), near, array], work


def share_owner(share, member):
    own = lax.axis_index("src")
    odd = own % 2
    first, second = FAR[0] + (FAR[1] - FAR[0]) * odd, FAR[1] + (FAR[0] - FAR[1]) * odd
    return own ^ (first, second ^ 1, 2, 0)[share] ^ member


def shards(
    flows, speeds, seg_length, relay_list, seg_slot, tile_pairs, tile_count, attenuation, dwellings
):
    sources, receivers = lax.axis_size("src"), lax.axis_size("rcv")
    hours = flows.shape[0]
    slots = sources * WIDTH
    f32, i32, bf16 = jnp.float32, jnp.int32, jnp.bfloat16
    blocks, facades = seg_slot.shape[0] // LANES, dwellings.shape[0] // LANES
    hours_weight = sum(
        1.0 if 7 <= h < 19 else (ROOT if 19 <= h < 23 else 10.0) for h in range(hours)
    )

    def vmem(shape, dtype):
        return (shape, dtype, "vmem")

    pairwise = sources == 8
    copies = 1 if pairwise else sources
    (power,) = call(
        functools.partial(source_kernel, copies),
        "source",
        [vmem((copies * BANDS, LANES), f32)],
        [(flows, "hbm"), (speeds, "hbm")],
        [
            pltpu.VMEM((hours, LANES), f32),
            pltpu.VMEM((hours, LANES), f32),
            pltpu.SemaphoreType.DMA((2,)),
        ],
    )
    tables, spread, ints, floats, people, tiles, pairs = call(
        prepare_kernel,
        "prepare",
        [
            vmem((2 * BANDS, hours, LANES), f32),
            vmem((blocks * LANES, slots), bf16),
            vmem((sources + blocks, LANES), i32),
            vmem((sources + blocks, LANES), f32),
            vmem((facades, LANES), i32),
            vmem(attenuation.shape[2:], bf16),
            (tile_pairs.shape[2:], i32, "smem"),
        ],
        [
            (array, "hbm")
            for array in (
                tile_pairs[0, 0],
                flows,
                speeds,
                seg_slot.reshape(blocks, LANES),
                relay_list[0],
                seg_length.reshape(blocks, LANES),
                dwellings.reshape(facades, LANES),
                attenuation[0, 0],
            )
        ],
        [
            pltpu.VMEM((hours, LANES), f32),
            pltpu.VMEM((hours, LANES), f32),
            pltpu.VMEM((sources, WIDTH), i32),
            pltpu.VMEM((sources, LANES), i32),
            pltpu.SemaphoreType.DMA((8,)),
        ],
    )
    if pairwise:
        power = jnp.concatenate([power, pair(power, 1)], axis=0)
        powers, (ints,) = exchange(power, [ints])
    else:
        powers = [lax.all_to_all(power, "src", 0, 0, tiled=True)]
    here = [(pairs, "smem"), (tile_count, "")]
    (part,) = call(
        functools.partial(forward_kernel, pairwise, copies),
        "forward",
        [vmem((copies * facades, LANES), f32)],
        here + [(array, "vmem") for array in (ints, floats, tiles, *powers)],
        [
            pltpu.VMEM((blocks, 2 * BANDS, LANES), bf16),
            pltpu.VMEM((facades, 2 * BANDS, LANES), f32),
        ],
    )
    (turned,) = call(
        turn_kernel,
        "turn",
        [vmem(attenuation.shape[2:], bf16)],
        [(tile_count, ""), (tiles, "vmem"), (part, "vmem")],
    )
    if pairwise:
        other, turned = lax.optimization_barrier((pair(part, 1), turned))
        total = part + other
        parts, _ = exchange(total, [])
    else:
        parts = [lax.all_to_all(part, "src", 0, 0, tiled=True)]
    (back,) = call(
        functools.partial(backward_kernel, hours, hours_weight, receivers),
        "backward",
        [vmem((receivers * sources * ROWS, LANES), f32)],
        here + [(array, "vmem") for array in (people, floats, spread, turned, *parts)],
        [
            pltpu.VMEM((facades, 32, LANES), bf16),
            pltpu.VMEM((blocks, 32, LANES), f32),
        ],
    )
    back = back.reshape(receivers * sources, ROWS, LANES)
    back = lax.all_to_all(back, ("rcv", "src"), 0, 0, tiled=True)
    back = back.reshape(receivers * sources * ROWS, LANES)
    grad_flows, grad_speeds, annoyed = call(
        functools.partial(finish_kernel, receivers),
        "finish",
        [((hours, LANES), f32, ""), ((hours, LANES), f32, ""), ((1, LANES), f32, "")],
        [(array, "vmem") for array in (back, tables)],
    )
    return grad_flows, grad_speeds, annoyed[0, 0]


def solution(mesh):
    in_specs = (
        P(None, "src"),
        P(None, "src"),
        P("src"),
        P("src", None, None),
        P("src"),
        P("src", "rcv", None, None),
        P("src", "rcv"),
        P("src", "rcv", None, None, None, None),
        P("rcv"),
    )
    out_specs = (P(None, "src"), P(None, "src"), P())
    return jax.shard_map(shards, mesh=mesh, in_specs=in_specs, out_specs=out_specs, check_vma=False)
```
